128 devices in a mesh: sample: 16 (over z, x_hi, core), variant: 8 (over y, x_lo).
Axes of the slice: x: 4 (x_hi: 2, x_lo: 2; x = x_hi * 2 + x_lo), y: 4, z: 4, core: 2. Of those that a mesh axis runs over, the one named last changes fastest.
Arguments:
- genotype: bfloat16 [32768, 16384], P('sample', 'variant'), may hold values from 0 to 2
- covariates: float32 [32768, 64], P('sample'), as said below
- outcome: float32 [32768, 256], P('sample', 'variant'), may hold values from 0 to 1
- cohort: int32 [32768], P('sample'), may hold values from 0 to 15
- measured: int32 [256, 16], P('variant'), may hold values from 0 to 1
Outputs:
- z_robust: float32 [256, 16384], P('sample', 'variant')
- z_model: float32 [256, 16384], P('sample', 'variant')
The draws below stay inside these ranges and needn't reach their ends.
Inputs may be any that keep to these rules, and one draw needn't show every extreme that they name: `covariates`: the first column is all ones.
All inputs are finite; a program needn't handle non-finite values.
Results may differ from the reference program's by a relative error of at most 0.004.
Values may be sent and summed in bfloat16 or wider, within the bound.
A program may use at most 128 MiB of HBM per device.

```python
import jax
import jax.numpy as jnp
from jax import lax

VAR_DEV = 2048
PHENOS = 256
COVARS = 64
COHORTS = 16
ITERS = 4
SAMPLES = 32768
VARIANTS = 16384


def covariate_table(key):
    values = jax.random.normal(key, (SAMPLES, COVARS), jnp.float32)
    column = jnp.arange(COVARS)[None, :]
    source = 1 + jnp.arange(COVARS) % 4
    shared = jnp.take(values, source, axis=1)
    mixed = jnp.where(column >= 5, 0.6 * shared + 0.8 * values, values)
    return jnp.where(column == 0, 1.0, mixed).astype(jnp.float32)


def draw_genotype(key, part):
    table = covariate_table(jax.random.fold_in(key, 11))
    strength = 0.6
    effects = jax.random.normal(jax.random.fold_in(key, 21), (4, VARIANTS), jnp.float32) * strength
    offset = jax.random.normal(jax.random.fold_in(key, 22), (VARIANTS,), jnp.float32) * 0.8
    linear = offset[None, :] + table[:, 1:2] * effects[0][None, :]
    linear = linear + table[:, 2:3] * effects[1][None, :]
    linear = linear + table[:, 3:4] * effects[2][None, :]
    linear = linear + table[:, 4:5] * effects[3][None, :]
    noise = jax.random.normal(jax.random.fold_in(key, 23), (SAMPLES, VARIANTS), jnp.float32)
    return (2.0 * jax.nn.sigmoid(linear + noise)).astype(jnp.bfloat16)


def draw_covariates(key, part):
    return covariate_table(jax.random.fold_in(key, 11))


def draw_outcome(key, part):
    table = covariate_table(jax.random.fold_in(key, 11))
    spread = 1.5
    effects = jax.random.normal(jax.random.fold_in(key, 12), (4, PHENOS), jnp.float32) * spread
    extra = jax.random.normal(jax.random.fold_in(key, 14), (4, PHENOS), jnp.float32) * (0.7 * spread)
    linear = table[:, 0:1] * effects[0][None, :]
    linear = linear + table[:, 1:2] * effects[1][None, :]
    linear = linear + table[:, 2:3] * effects[2][None, :]
    linear = linear + table[:, 3:4] * effects[3][None, :]
    for column_index in range(4):
        start = COVARS - 4 + column_index
        linear = linear + table[:, start:start + 1] * extra[column_index][None, :]
    noise = jax.random.normal(jax.random.fold_in(key, 13), (SAMPLES, PHENOS), jnp.float32) * 1.5
    return jax.nn.sigmoid(linear + noise).astype(jnp.float32)


def draw_cohort(key, part):
    base = jnp.arange(SAMPLES, dtype=jnp.int32) * COHORTS // SAMPLES
    jitter = jax.random.randint(key, (SAMPLES,), 0, 2, dtype=jnp.int32)
    return jnp.minimum(base + jitter, COHORTS - 1).astype(jnp.int32)


def draw_measured(key, part):
    level = jnp.arange(COHORTS, dtype=jnp.int32)[None, :]
    tickets = jax.random.randint(key, (PHENOS, COHORTS), 0, 4 * COHORTS, dtype=jnp.int32)
    return (tickets < COHORTS + 3 * level + 3).astype(jnp.int32)


def setup_inputs(seed: int = 0) -> dict:
    seeds = jax.random.split(jax.random.key(seed), 6)
    genotype = draw_genotype(jax.random.fold_in(seeds[5], 71), 0)
    covariates = draw_covariates(jax.random.fold_in(seeds[5], 71), 0)
    outcome = draw_outcome(jax.random.fold_in(seeds[5], 71), 0)
    cohort = draw_cohort(jax.random.fold_in(seeds[5], 71), 0)
    measured = draw_measured(jax.random.fold_in(seeds[5], 71), 0)
    return dict(genotype=genotype, covariates=covariates, outcome=outcome, cohort=cohort, measured=measured)


epsilon = 1e-06
highest = lax.Precision.HIGHEST

def curvature(covariates, weights):
    blocks = weights.T.reshape(PHENOS // 16, 16, covariates.shape[0])

    def one_block(block):
        return jnp.einsum('pn,nc,nd->pcd', block, covariates, covariates, precision=highest)
    return lax.map(one_block, blocks).reshape(PHENOS, COVARS, COVARS)

def reference(genotype, covariates, outcome, cohort, measured):
    onehot = (cohort[:, None] == jnp.arange(COHORTS, dtype=jnp.int32)[None, :]).astype(jnp.float32)
    mask = jnp.dot(onehot, measured.T.astype(jnp.float32), precision=highest)
    beta = jnp.zeros((PHENOS, COVARS), jnp.float32)
    for step_index in range(ITERS):
        linear = jnp.dot(covariates, beta.T, precision=highest)
        fitted = jax.nn.sigmoid(linear)
        weights = mask * fitted * (1.0 - fitted)
        working = mask * (outcome - fitted)
        hess = curvature(covariates, weights)
        grad = jnp.dot(working.T, covariates, precision=highest)
        beta = beta + jnp.linalg.solve(hess, grad[..., None])[..., 0]
    linear = jnp.dot(covariates, beta.T, precision=highest)
    fitted = jax.nn.sigmoid(linear)
    resid = (mask * (outcome - fitted)).astype(jnp.bfloat16)
    wslab = (mask * fitted * (1.0 - fitted)).astype(jnp.bfloat16)
    resid_sq = (resid.astype(jnp.float32) ** 2).astype(jnp.bfloat16)
    gram = jnp.dot(covariates.T, covariates, precision=highest)
    nblocks = VARIANTS // VAR_DEV
    blocks = genotype.reshape(SAMPLES, nblocks, VAR_DEV).transpose(1, 0, 2)

    def one_block(block):
        dosage = block.astype(jnp.float32)
        cross = jnp.dot(covariates.T, dosage, precision=highest)
        coef = jnp.linalg.solve(gram, cross)
        proj = dosage - jnp.dot(covariates, coef, precision=highest)
        proj_b = proj.astype(jnp.bfloat16)
        proj_sq = (proj * proj).astype(jnp.bfloat16)
        score = jnp.dot(resid.T.astype(jnp.float32), proj_b.astype(jnp.float32), preferred_element_type=jnp.float32)
        robust = jnp.dot(resid_sq.T.astype(jnp.float32), proj_sq.astype(jnp.float32), preferred_element_type=jnp.float32)
        model = jnp.dot(wslab.T.astype(jnp.float32), proj_sq.astype(jnp.float32), preferred_element_type=jnp.float32)
        return (score / jnp.sqrt(robust + epsilon), score / jnp.sqrt(model + epsilon))
    first, second = lax.map(one_block, blocks)
    z_robust = first.transpose(1, 0, 2).reshape(PHENOS, VARIANTS)
    z_model = second.transpose(1, 0, 2).reshape(PHENOS, VARIANTS)
    return (z_robust, z_model)
```

```python
import functools

import jax
import jax.numpy as jnp
from jax import lax
from jax.experimental import pallas as pl
from jax.experimental.pallas import tpu as pltpu
from jax.sharding import PartitionSpec as P

ITERS = 4
EPS = 1e-06
HIGHEST = lax.Precision.HIGHEST
F32 = jnp.float32
BF16 = jnp.bfloat16
TILES = 4
PROJ = 256
ROWS = 512


def dot(a, b):
    return jnp.dot(a, b, preferred_element_type=F32)


def exact(a, b):
    return jnp.dot(a, b, preferred_element_type=F32, precision=HIGHEST)


def two(x):
    hi = x.astype(BF16)
    return hi, (x - hi.astype(F32)).astype(BF16)


def fold(x):
    return x + pltpu.roll(x, 64, 1)


def eta_of(rows, xt2):
    low = lax.broadcasted_iota(jnp.int32, rows.shape, 1) < 64
    zero = jnp.zeros_like(rows)
    beta = jnp.concatenate([jnp.where(low, rows, zero), jnp.where(low, zero, rows)], axis=0)
    return exact(beta, xt2)


def sweep(m, g):
    lane = lax.broadcasted_iota(jnp.int32, (1, 128), 1)
    low = lane < 64
    grow = lax.broadcasted_iota(jnp.int32, (64, 1), 0)
    for k in range(64):
        if k % 8 == 0 and k:
            m = m[8:, :]
        r = k % 8
        at = (lane == k) | (lane == k + 64)
        col = jnp.where(low, m[:, k : k + 1], m[:, 64 + k : 65 + k])
        inv = 1.0 / col[r : r + 1, :]
        row = jnp.where(at, -1.0, m[r : r + 1, :]) * inv
        m = jnp.where(at, 0.0, m) - col * row
        if g is not None:
            gcol = jnp.broadcast_to(g[:, k : k + 1], g.shape)
            ginv = 1.0 / gcol[k : k + 1, :]
            gline = jnp.where(at, -1.0, g[k : k + 1, :]) * ginv
            here = grow == k
            g = jnp.where(at | here, 0.0, g) - jnp.where(here, -1.0, gcol) * gline
    return m[8:9, :], g


def kernel(
    ns,
    nv,
    g_hbm,
    xt2_ref,
    x4_ref,
    y_ref,
    zr_ref,
    zm_ref,
    gbuf,
    psq,
    xhl,
    yall,
    wbuf,
    rsp,
    lhs,
    hs,
    hr,
    crs,
    crr,
    grs,
    grr,
    ginv_ref,
    bcur,
    br,
    ball,
    c4,
    cfall,
    r1,
    r2,
    so,
    asd,
    arv,
    bsd,
    brv,
    fin,
    g_sem,
    h_ss,
    h_rs,
    c_ss,
    c_rs,
    gr_ss,
    gr_rs,
    b_ss,
    b_rs,
    f_ss,
    f_rs,
    y_ss,
    y_rs,
    v_ss,
    v_rs,
    a_ss,
    a_rs,
    q_ss,
    q_rs,
):
    s = lax.axis_index("sample")
    v = lax.axis_index("variant")
    core = lax.rem(s, 2)
    myq = s // 2
    low = lax.broadcasted_iota(jnp.int32, (1, 128), 1) < 64

    gcopy = pltpu.make_async_copy(g_hbm, gbuf, g_sem)
    gcopy.start()

    def speer(d):
        return lax.rem(s + d, ns)

    def vpeer(d):
        return lax.rem(v + d, nv)

    def remote(src, dst, ss, rs, sample, variant):
        return pltpu.make_async_remote_copy(
            src_ref=src,
            dst_ref=dst,
            send_sem=ss,
            recv_sem=rs,
            device_id=(sample, variant),
            device_id_type=pl.DeviceIdType.MESH,
        )

    barrier = pltpu.get_barrier_semaphore()

    @pl.loop(1, ns)
    def _(d):
        pl.semaphore_signal(
            barrier, inc=1, device_id=(speer(d), v), device_id_type=pl.DeviceIdType.MESH
        )

    @pl.loop(1, nv)
    def _(d):
        pl.semaphore_signal(
            barrier, inc=1, device_id=(s, vpeer(d)), device_id_type=pl.DeviceIdType.MESH
        )

    hi, lo = two(xt2_ref[0:64, :])
    xhl[0:64, :] = hi
    xhl[64:128, :] = lo
    bcur[...] = jnp.zeros_like(bcur)
    br[...] = jnp.zeros_like(br)
    hs[...] = jnp.zeros_like(hs)
    grams = dot(xhl[...], x4_ref[:, 0:128])
    grs[...] = fold(grams[0:64, :] + grams[64:128, :])

    pl.semaphore_wait(barrier, ns + nv - 2)

    def y_copy(j):
        return remote(y_ref, yall.at[v], y_ss.at[j], y_rs.at[v], s, j)

    def y_from(j):
        return remote(y_ref, yall.at[j], y_ss.at[j], y_rs.at[j], s, j)

    def gr_copy(j):
        return remote(grs, grr.at[s], gr_ss.at[j], gr_rs.at[s], j, v)

    def gr_from(j):
        return remote(grs, grr.at[j], gr_ss.at[j], gr_rs.at[j], j, v)

    def h_copy(j):
        return remote(hs.at[j], hr.at[s], h_ss.at[j], h_rs.at[s], j, v)

    def h_from(j):
        return remote(hs.at[j], hr.at[j], h_ss.at[j], h_rs.at[j], j, v)

    def c_copy(j):
        return remote(crs.at[j], crr.at[s], c_ss.at[j], c_rs.at[s], j, v)

    def c_from(j):
        return remote(crs.at[j], crr.at[j], c_ss.at[j], c_rs.at[j], j, v)

    def b_copy(j):
        return remote(br.at[s], br.at[s], b_ss.at[j], b_rs.at[s], j, v)

    def b_from(j):
        return remote(br.at[s], br.at[j], b_ss.at[j], b_rs.at[j], j, v)

    def f_copy(j):
        return remote(cfall.at[s], cfall.at[s], f_ss.at[j], f_rs.at[s], j, v)

    def f_from(j):
        return remote(cfall.at[s], cfall.at[j], f_ss.at[j], f_rs.at[j], j, v)

    def v_copy(j):
        return remote(ball.at[v], ball.at[v], v_ss.at[j], v_rs.at[v], s, j)

    def v_from(j):
        return remote(ball.at[v], ball.at[j], v_ss.at[j], v_rs.at[j], s, j)

    def each(n, peer, do):
        @pl.loop(1, n)
        def _(d):
            do(peer(d))

    each(ns, speer, lambda j: gr_copy(j).start())
    each(nv, vpeer, lambda j: y_copy(j).start())

    def hessians():
        eta = eta_of(br[:, 0, :], xt2_ref[...])
        fitted = 1.0 / (1.0 + jnp.exp(-eta))
        coded = y_ref[...]
        seen = coded >= 0.0
        wbuf[...] = jnp.where(seen, fitted * (1.0 - fitted), 0.0)
        work = jnp.where(seen, coded - fitted, 0.0)
        r_hi = work.astype(BF16)
        rest = work - r_hi.astype(F32)
        r_mid, r_lo = two(rest)
        rsp[0:32, :] = r_hi
        rsp[32:64, :] = r_mid
        rsp[64:96, :] = r_lo
        gsum = dot(rsp[...], x4_ref[:, 0:128])
        gsum = fold(gsum[0:32] + gsum[32:64] + gsum[64:96])
        gpair = jnp.where(low, gsum[0:16], gsum[16:32])
        for j in range(16):
            hs[j, 64:65, :] = gpair[j : j + 1]

        @pl.loop(0, 4)
        def _(group):
            @pl.loop(0, 4)
            def _(i):
                for half in range(2):
                    w = wbuf[pl.ds(group * 4 + i + 16 * half, 1), :]
                    base = pl.multiple_of(i * 256 + half * 128, 128)
                    for c in range(4):
                        cols = slice(c * 512, (c + 1) * 512)
                        hi, lo = two(xt2_ref[0:64, cols] * w[:, cols])
                        lhs[pl.ds(base, 64), cols] = hi
                        lhs[pl.ds(base + 64, 64), cols] = lo

            out = dot(lhs[...], x4_ref[:, 0:128])
            for i in range(4):
                part = out[i * 256 : (i + 1) * 256]
                first = fold(part[0:64] + part[64:128])
                second = fold(part[128:192] + part[192:256])
                hs[group * 4 + i, 0:64, :] = jnp.where(low, first, second)

    def crosses():
        @pl.loop(0, 8)
        def _(t):
            out = dot(xhl[...], gbuf[:, pl.ds(pl.multiple_of(t * 256, 256), 256)])
            out = out[0:64] + out[64:128]
            crs[2 * t] = out[:, 0:128]
            crs[2 * t + 1] = out[:, 128:256]

    def project(t):
        for h in range(2):
            part = cfall[2 * t + h]
            cols = slice(h * 128, (h + 1) * 128)
            c4[0:64, cols] = part[0:64]
            c4[64:128, cols] = part[0:64]
            c4[128:192, cols] = part[64:128]
            c4[192:256, cols] = part[64:128]
        cols = pl.ds(pl.multiple_of(t * PROJ, PROJ), PROJ)

        @pl.loop(0, 2048 // ROWS)
        def _(i):
            rows = pl.ds(pl.multiple_of(i * ROWS, ROWS), ROWS)
            proj = gbuf[rows, cols].astype(F32) - dot(x4_ref[rows, :], c4[...])
            gbuf[rows, cols] = proj.astype(BF16)
            psq[rows, cols] = (proj * proj).astype(BF16)

    @pl.loop(0, ITERS)
    def _(it):
        hessians()
        each(ns, speer, lambda j: h_copy(j).start())

        @pl.when(it == 0)
        def _():
            gcopy.wait()
            crosses()
            each(ns, speer, lambda j: c_copy(j).start())
            each(ns, speer, lambda j: gr_from(j).wait_recv())
            grr[s] = grs[...]
            total = grr[0]
            for j in range(1, ns):
                total = total + grr[j]
            ginv_ref[...] = total

        @pl.when(it == 1)
        def _():
            each(ns, speer, lambda j: f_from(j).wait_recv())

        @pl.when(it >= 1)
        def _():
            @pl.loop((it - 1) * 3, jnp.minimum(it * 3, 2048 // PROJ))
            def _(t):
                project(t)

        each(ns, speer, lambda j: h_from(j).wait_recv())
        hr[s] = hs[s]
        total = hr[0]
        for j in range(1, ns):
            total = total + hr[j]
        delta, ginv = sweep(total, ginv_ref[...])
        bcur[0:1, :] = bcur[0:1, :] + delta

        @pl.when(it > 0)
        def _():
            each(ns, speer, lambda j: b_copy(j).wait_send())

        br[s] = bcur[...]
        each(ns, speer, lambda j: b_copy(j).start())

        @pl.when(it == 0)
        def _():
            each(ns, speer, lambda j: c_from(j).wait_recv())
            crr[s] = crs[s]
            cross = crr[0]
            for j in range(1, ns):
                cross = cross + crr[j]
            hi, lo = two(exact(-ginv[:, 0:64], cross))
            cfall[s, 0:64, :] = hi
            cfall[s, 64:128, :] = lo
            each(ns, speer, lambda j: f_copy(j).start())

        each(ns, speer, lambda j: h_copy(j).wait_send())
        each(ns, speer, lambda j: b_from(j).wait_recv())

    each(ns, speer, lambda j: b_copy(j).wait_send())
    ball[v] = br[:, 0, :]
    each(nv, vpeer, lambda j: v_copy(j).start())
    each(nv, vpeer, lambda j: y_from(j).wait_recv())
    yall[v] = y_ref[...]
    each(nv, vpeer, lambda j: v_from(j).wait_recv())

    @pl.loop(0, nv)
    def _(u):
        eta = eta_of(ball[u], xt2_ref[...])
        fitted = 1.0 / (1.0 + jnp.exp(-eta))
        coded = yall[u]
        seen = coded >= 0.0
        resid = jnp.where(seen, coded - fitted, 0.0).astype(BF16)
        wslab = jnp.where(seen, fitted * (1.0 - fitted), 0.0).astype(BF16)
        wide = resid.astype(F32)
        square = (wide * wide).astype(BF16)
        for h in range(2):
            half = slice(h * 16, (h + 1) * 16)
            at = pl.multiple_of(u * 16 + h * 128, 16)
            r1[pl.ds(at, 16), :] = resid[half]
            r2[pl.ds(at, 16), :] = square[half]
            r2[pl.ds(at + 256, 16), :] = wslab[half]

    width = 2048 // TILES

    def a_copy(t):
        return remote(asd.at[t], arv.at[t], a_ss.at[t], a_rs.at[t], s + 1 - 2 * core, v)

    def q_copy(t, q):
        return remote(bsd.at[t, q], brv.at[t, myq], q_ss.at[t, q], q_rs.at[t, myq], 2 * q + core, v)

    def q_from(t, q):
        return remote(bsd.at[t, q], brv.at[t, q], q_ss.at[t, q], q_rs.at[t, q], 2 * q + core, v)

    def others(do):
        @pl.loop(1, ns // 2)
        def _(d):
            do(lax.rem(myq + d, ns // 2))

    @pl.loop(0, TILES + 1)
    def _(t):
        @pl.when(t < TILES)
        def _():
            slot = lax.rem(t, 2)
            cols = pl.ds(pl.multiple_of(t * width, width), width)
            so[slot, 0:256, :] = dot(r1[...], gbuf[:, cols])
            so[slot, 256:768, :] = dot(r2[...], psq[:, cols])

            @pl.loop(0, ns // 2)
            def _(q):
                at = pl.multiple_of((1 - core) * 128 + q * 16, 16)
                hi, lo = two(so[slot, pl.ds(at, 16), :])
                asd[t, q, 0:16, :] = hi
                asd[t, q, 16:32, :] = lo
                asd[t, q, 32:48, :] = so[slot, pl.ds(at + 256, 16), :].astype(BF16)
                asd[t, q, 48:64, :] = so[slot, pl.ds(at + 512, 16), :].astype(BF16)

            a_copy(t).start()

        @pl.when(t > 0)
        def _():
            b = t - 1
            slot = lax.rem(b, 2)
            a_copy(b).wait_recv()

            def total(q):
                at = pl.multiple_of(core * 128 + q * 16, 16)
                score = so[slot, pl.ds(at, 16), :]
                score = score + arv[b, q, 0:16, :].astype(F32) + arv[b, q, 16:32, :].astype(F32)
                robust = so[slot, pl.ds(at + 256, 16), :] + arv[b, q, 32:48, :].astype(F32)
                model = so[slot, pl.ds(at + 512, 16), :] + arv[b, q, 48:64, :].astype(F32)
                return score, robust, model

            def send(q):
                score, robust, model = total(q)
                hi, lo = two(score)
                bsd[b, q, 0:16, :] = hi
                bsd[b, q, 16:32, :] = lo
                bsd[b, q, 32:48, :] = robust.astype(BF16)
                bsd[b, q, 48:64, :] = model.astype(BF16)
                q_copy(b, q).start()

            others(send)
            score, robust, model = total(myq)
            fin[b, 0:16, :] = score
            fin[b, 16:32, :] = robust
            fin[b, 32:48, :] = model

    for t in range(TILES):
        others(lambda q: q_from(t, q).wait_recv())
        brv[t, myq] = jnp.zeros((64, width), BF16)
        score, robust, model = fin[t, 0:16, :], fin[t, 16:32, :], fin[t, 32:48, :]
        for q in range(ns // 2):
            score = score + brv[t, q, 0:16, :].astype(F32) + brv[t, q, 16:32, :].astype(F32)
            robust = robust + brv[t, q, 32:48, :].astype(F32)
            model = model + brv[t, q, 48:64, :].astype(F32)
        cols = slice(t * width, (t + 1) * width)
        zr_ref[:, cols] = score * lax.rsqrt(robust + EPS)
        zm_ref[:, cols] = score * lax.rsqrt(model + EPS)

    each(ns, speer, lambda j: gr_copy(j).wait_send())
    each(ns, speer, lambda j: c_copy(j).wait_send())
    each(ns, speer, lambda j: f_copy(j).wait_send())
    each(nv, vpeer, lambda j: y_copy(j).wait_send())
    each(nv, vpeer, lambda j: v_copy(j).wait_send())

    @pl.loop(0, TILES)
    def _(t):
        a_copy(t).wait_send()
        others(lambda q: q_copy(t, q).wait_send())


def per_device(ns, nv, genotype, covariates, outcome, cohort, measured):
    rows = covariates.shape[0]
    cohorts = measured.shape[1]
    onehot = (jnp.arange(cohorts, dtype=jnp.int32)[:, None] == cohort[None, :]).astype(BF16)
    mask = jnp.dot(measured.astype(BF16), onehot, preferred_element_type=F32)
    coded = jnp.where(mask > 0.5, outcome.T, -1.0)
    xt = covariates.T
    xt2 = jnp.concatenate([xt, xt], axis=0)
    xh = lax.reduce_precision(covariates, 8, 7)
    xl = covariates - xh
    x4 = jnp.concatenate([xh, xl, xh, xl], axis=1).astype(BF16)
    out = jax.ShapeDtypeStruct((256 // ns, 2048), F32)
    vm = pltpu.VMEM
    dma = pltpu.SemaphoreType.DMA
    width = 2048 // TILES
    scratch = [
        vm((2048, 2048), BF16),
        vm((2048, 2048), BF16),
        vm((128, 2048), BF16),
        vm((nv, 32, 2048), F32),
        vm((32, 2048), F32),
        vm((96, 2048), BF16),
        vm((1024, 2048), BF16),
        vm((ns, 72, 128), F32),
        vm((ns, 72, 128), F32),
        vm((ns, 64, 128), F32),
        vm((ns, 64, 128), F32),
        vm((64, 128), F32),
        vm((ns, 64, 128), F32),
        vm((64, 128), F32),
        vm((8, 128), F32),
        vm((ns, 8, 128), F32),
        vm((nv, 16, 128), F32),
        vm((256, PROJ), BF16),
        vm((ns, 128, 128), BF16),
        vm((256, 2048), BF16),
        vm((512, 2048), BF16),
        vm((2, 768, width), F32),
        vm((TILES, ns // 2, 64, width), BF16),
        vm((TILES, ns // 2, 64, width), BF16),
        vm((TILES, ns // 2, 64, width), BF16),
        vm((TILES, ns // 2, 64, width), BF16),
        vm((TILES, 48, width), F32),
        dma,
    ]
    scratch += [dma((ns,))] * 10 + [dma((nv,))] * 4 + [dma((TILES,))] * 2
    scratch += [dma((TILES, ns // 2))] * 2
    return pl.pallas_call(
        functools.partial(kernel, ns, nv),
        out_shape=(out, out),
        in_specs=[pl.BlockSpec(memory_space=pl.ANY)] + [pl.BlockSpec(memory_space=pltpu.VMEM)] * 3,
        out_specs=(pl.BlockSpec(memory_space=pltpu.VMEM),) * 2,
        scratch_shapes=scratch,
        compiler_params=pltpu.CompilerParams(
            collective_id=0, has_side_effects=True, vmem_limit_bytes=60 * 2**20
        ),
        name="score_tests",
    )(genotype, xt2, x4, coded)


def solution(mesh):
    placed = (
        P("sample", "variant"),
        P("sample", None),
        P("sample", "variant"),
        P("sample"),
        P("variant", None),
    )
    return jax.shard_map(
        functools.partial(per_device, mesh.shape["sample"], mesh.shape["variant"]),
        mesh=mesh,
        in_specs=placed,
        out_specs=(P("sample", "variant"), P("sample", "variant")),
        check_vma=False,
    )
```

```python
import functools

import jax
import jax.numpy as jnp
from jax import lax
from jax.experimental import pallas as pl
from jax.experimental.pallas import tpu as pltpu
from jax.sharding import PartitionSpec as P

ITERS = 4
EPS = 1e-06
HIGHEST = lax.Precision.HIGHEST
F32 = jnp.float32
BF16 = jnp.bfloat16
TILES = 4
PROJ = 256
ROWS = 512


def dot(a, b):
    return jnp.dot(a, b, preferred_element_type=F32)


def exact(a, b):
    return jnp.dot(a, b, preferred_element_type=F32, precision=HIGHEST)


def two(x):
    hi = x.astype(BF16)
    return hi, (x - hi.astype(F32)).astype(BF16)


def fold(x):
    return x + pltpu.roll(x, 64, 1)


def exact_t(a, b):
    return lax.dot_general(a, b, (((1,), (1,)), ((), ())), preferred_element_type=F32)


def product(x, y):
    out = []
    for i in range(len(x)):
        line = []
        for j in range(len(y[0])):
            term = x[i][0] * y[0][j]
            for k in range(1, len(y)):
                term = term + x[i][k] * y[k][j]
            line.append(term)
        out.append(line)
    return out


def inverse2(a):
    (p, q), (_, d) = a
    i = 1.0 / (p * d - q * q)
    return [[d * i, -(q * i)], [-(q * i), p * i]]


def inverse4(a):
    right = [r[2:] for r in a[:2]]
    corner = [r[2:] for r in a[2:]]
    flip = lambda x: [list(c) for c in zip(*x)]
    first = inverse2([r[:2] for r in a[:2]])
    lead = product(first, right)
    inner = product(flip(right), lead)
    last = inverse2([[corner[i][j] - inner[i][j] for j in range(2)] for i in range(2)])
    side = product(lead, last)
    more = product(side, flip(lead))
    top = [[first[i][j] + more[i][j] for j in range(2)] + [-side[i][j] for j in range(2)] for i in range(2)]
    return top + [[-side[j][i] for j in range(2)] + last[i] for i in range(2)]


def sweep(m, full):
    lane = lax.broadcasted_iota(jnp.int32, (1, 128), 1)
    low = lane < 64
    place = jnp.where(low, lane, lane - 64)
    height = lax.broadcasted_iota(jnp.int32, (64, 1), 0)
    for k in range(0, 64, 4):
        if not full and k % 8 == 0 and k:
            m = m[8:, :]
        r = k if full else k % 8
        cols = [jnp.where(low, m[:, k + j : k + j + 1], m[:, 64 + k + j : 65 + k + j]) for j in range(4)]
        pivot = [[cols[max(i, j)][r + min(i, j) : r + min(i, j) + 1, :] for j in range(4)] for i in range(4)]
        here = (place >= k) & (place < k + 4)
        lines = [
            [jnp.where(here, jnp.where(place == k + j, -1.0, 0.0), m[r + j : r + j + 1, :])] for j in range(4)
        ]
        lines = product(inverse4(pivot), lines)
        m = jnp.where(here, 0.0, m)
        if full:
            mine = (height >= k) & (height < k + 4)
            m = jnp.where(mine, 0.0, m)
            cols = [jnp.where(mine, jnp.where(height == k + j, -1.0, 0.0), cols[j]) for j in range(4)]
        m = m - product([cols], lines)[0][0]
    return m if full else m[8:9, :]


def kernel(
    ns,
    nv,
    g_hbm,
    xt_ref,
    out_ref,
    cohort_ref,
    meas_ref,
    tot_ref,
    gbuf,
    psq,
    xt4,
    xhl,
    x4,
    ybuf,
    y4,
    yall,
    wbuf,
    lhs,
    hacc,
    hs,
    hr,
    crs,
    crr,
    grs,
    grr,
    ginv_ref,
    bcur,
    br,
    bet,
    ball,
    c4,
    cfall,
    r1,
    r2,
    so,
    asd,
    arv,
    bsd,
    brv,
    fin,
    g_sem,
    c_ss,
    c_rs,
    f_ss,
    f_rs,
    h_ss,
    h_rs,
    gr_ss,
    gr_rs,
    b_ss,
    b_rs,
    x_ss,
    x_rs,
    p_ss,
    p_rs,
    y_ss,
    y_rs,
    v_ss,
    v_rs,
    a_ss,
    a_rs,
    q_ss,
    q_rs,
):
    nz = ns // 4
    s = lax.axis_index("sample")
    v = lax.axis_index("variant")
    z = s // 4
    sub = lax.rem(s, 4)
    core = lax.rem(s, 2)
    xh = sub // 2
    myq = s // 2
    sibling = s + 1 - 2 * core
    across = s + 2 - 4 * xh
    near = v + 1 - 2 * lax.rem(v, 2)
    low = lax.broadcasted_iota(jnp.int32, (1, 128), 1) < 64
    mesh_id = pl.DeviceIdType.MESH

    gcopy = pltpu.make_async_copy(g_hbm, gbuf, g_sem)
    gcopy.start()

    def block(b):
        return pl.ds(pl.multiple_of(b * 2048, 2048), 2048)

    def split(b):
        hi, lo = two(xt4[:, block(b)])
        xhl[0:64, block(b)] = hi
        xhl[64:128, block(b)] = lo

    def block_at(i):
        return 2 * lax.rem(xh + i // 2, 2) + lax.rem(core + i, 2)

    def speer(d):
        return lax.rem(s + d, ns)

    def zpeer(d):
        return lax.rem(z + d, nz)

    def vpeer(d):
        return lax.rem(v + d, nv)

    def remote(src, dst, ss, rs, sample, variant):
        return pltpu.make_async_remote_copy(
            src_ref=src,
            dst_ref=dst,
            send_sem=ss,
            recv_sem=rs,
            device_id=(sample, variant),
            device_id_type=mesh_id,
        )

    def each(n, peer, do):
        @pl.loop(1, n)
        def _(d):
            do(peer(d))

    barrier = pltpu.get_barrier_semaphore()

    def greet(sample, variant):
        pl.semaphore_signal(barrier, inc=1, device_id=(sample, variant), device_id_type=mesh_id)

    plane = 4 * nv
    place = v * 4 + sub

    def ppeer(d):
        return lax.rem(place + d, plane)

    @pl.loop(1, nz)
    def _(d):
        for k in range(4):
            greet(4 * zpeer(d) + k, v)

    each(plane, ppeer, lambda j: greet(4 * z + lax.rem(j, 4), j // 4))

    hot = lax.broadcasted_iota(jnp.int32, (16, 2048), 0) == cohort_ref[...]
    mask = lax.dot_general(
        meas_ref[...].astype(BF16),
        hot.astype(BF16),
        (((0,), (0,)), ((), ())),
        preferred_element_type=F32,
    )
    ybuf[...] = jnp.where(mask > 0.5, out_ref[...], -1.0)
    own = block(sub)
    y4[:, own] = ybuf[pl.ds(pl.multiple_of(sub * 8, 8), 8), :]
    xt4[:, own] = xt_ref[...]
    split(sub)
    bcur[...] = jnp.zeros_like(bcur)
    br[...] = jnp.zeros_like(br)
    bet[...] = jnp.zeros_like(bet)
    hs[...] = jnp.zeros_like(hs)

    pl.semaphore_wait(barrier, 4 * (nz - 1) + plane - 1)

    def x_beside():
        return remote(xt_ref, xt4.at[:, own], x_ss.at[1], x_rs.at[1], sibling, v)

    def x_across():
        return remote(xt_ref, xt4.at[:, own], x_ss.at[2], x_rs.at[2], across, near)

    def x_relay():
        b = block(block_at(2))
        return remote(xt4.at[:, b], xt4.at[:, b], x_ss.at[3], x_rs.at[3], sibling, v)

    def x_from(i):
        b = block(block_at(i))
        return remote(xt_ref, xt4.at[:, b], x_ss.at[i], x_rs.at[i], sibling, v)

    def p_copy(j):
        rows = pl.ds(pl.multiple_of(j * 8, 8), 8)
        return remote(ybuf.at[rows], y4.at[:, own], p_ss.at[j], p_rs.at[sub], 4 * z + j, v)

    def p_from(j):
        rows = pl.ds(pl.multiple_of(j * 8, 8), 8)
        return remote(ybuf.at[rows], y4.at[:, block(j)], p_ss.at[j], p_rs.at[j], 4 * z + j, v)

    def y_copy(j):
        return remote(ybuf, yall.at[v], y_ss.at[j], y_rs.at[v], s, j)

    def y_from(j):
        return remote(ybuf, yall.at[j], y_ss.at[j], y_rs.at[j], s, j)

    def gr_copy(j):
        return remote(grs, grr.at[z], gr_ss.at[j], gr_rs.at[z], 4 * j + sub, v)

    def gr_from(j):
        return remote(grs, grr.at[j], gr_ss.at[j], gr_rs.at[j], 4 * j + sub, v)

    def h_copy(j):
        return remote(hs.at[j], hr.at[z], h_ss.at[j], h_rs.at[z], 4 * j + sub, v)

    def h_from(j):
        return remote(hs.at[j], hr.at[j], h_ss.at[j], h_rs.at[j], 4 * j + sub, v)

    def b_copy(j):
        return remote(br.at[z], br.at[z], b_ss.at[j], b_rs.at[z], 4 * j + sub, v)

    def b_from(j):
        return remote(br.at[z], br.at[j], b_ss.at[j], b_rs.at[j], 4 * j + sub, v)

    def c_copy(j):
        return remote(crs.at[j], crr.at[s], c_ss.at[j], c_rs.at[s], j, v)

    def c_from(j):
        return remote(crs.at[j], crr.at[j], c_ss.at[j], c_rs.at[j], j, v)

    def f_copy(j):
        return remote(cfall.at[s], cfall.at[s], f_ss.at[j], f_rs.at[s], j, v)

    def f_from(j):
        return remote(cfall.at[s], cfall.at[j], f_ss.at[j], f_rs.at[j], j, v)

    def v_copy(j):
        to = 4 * z + lax.rem(j, 4)
        mine = ball.at[place]
        return remote(mine, mine, v_ss.at[j], v_rs.at[place], to, j // 4)

    def v_from(j):
        to = 4 * z + lax.rem(j, 4)
        return remote(ball.at[place], ball.at[j], v_ss.at[j], v_rs.at[j], to, j // 4)

    x_across().start()
    x_beside().start()
    each(4, lambda i: block_at(i), lambda j: p_copy(j).start())

    def products():
        beta = bet[:, 0:64]
        b_hi = beta.astype(BF16).astype(F32)
        rest = beta - b_hi
        b_mid = rest.astype(BF16).astype(F32)
        none = jnp.zeros_like(beta)
        rows = jnp.concatenate([b_hi, b_mid, rest - b_mid, none], axis=0)
        rows = jnp.concatenate([rows, rows], axis=1).astype(BF16)
        eta = dot(rows, xhl[...])
        eta = eta[0:8] + eta[8:16] + eta[16:24]
        fitted = 1.0 / (1.0 + jnp.exp(-eta))
        coded = y4[...]
        seen = coded >= 0.0
        wbuf[...] = jnp.where(seen, fitted * (1.0 - fitted), 0.0)
        work = jnp.where(seen, coded - fitted, 0.0)
        r_hi = work.astype(BF16).astype(F32)
        rest = work - r_hi
        r_mid = rest.astype(BF16).astype(F32)
        none = jnp.zeros_like(work)
        lhs[512:544, :] = jnp.concatenate([r_hi, r_mid, rest - r_mid, none], axis=0).astype(BF16)

        @pl.loop(0, 16)
        def _(i):
            cols = pl.ds(pl.multiple_of(i * 512, 512), 512)
            table = xt4[:, cols]
            for p in range(8):
                lhs[p * 64 : (p + 1) * 64, cols] = (table * wbuf[p : p + 1, cols]).astype(BF16)

        hacc[...] = exact_t(lhs[...], xhl[...])

    def pack():
        def one(p):
            return fold(hacc[p * 64 : (p + 1) * 64, :])

        grads = fold(hacc[512:520, :] + hacc[520:528, :] + hacc[528:536, :])
        for j in range(nz):
            hs[j, 0:64, :] = jnp.where(low, one(j), one(j + nz))
            hs[j, 64:65, :] = jnp.where(low, grads[j : j + 1], grads[j + nz : j + nz + 1])

    def crosses():
        @pl.loop(0, 8)
        def _(t):
            out = dot(xhl[:, own], gbuf[:, pl.ds(pl.multiple_of(t * 256, 256), 256)])
            out = out[0:64] + out[64:128]
            crs[2 * t] = out[:, 0:128]
            crs[2 * t + 1] = out[:, 128:256]

    def upright():
        @pl.loop(0, 16)
        def _(i):
            at = pl.ds(pl.multiple_of(i * 128, 128), 128)
            from_ = pl.ds(pl.multiple_of(sub * 2048 + i * 128, 128), 128)
            both = xhl[:, from_].astype(F32).T.astype(BF16)
            x4[at, 0:128] = both
            x4[at, 128:256] = both

    def project(t):
        for h in range(2):
            part = cfall[2 * t + h]
            cols = slice(h * 128, (h + 1) * 128)
            c4[0:64, cols] = part[0:64]
            c4[64:128, cols] = part[0:64]
            c4[128:192, cols] = part[64:128]
            c4[192:256, cols] = part[64:128]
        cols = pl.ds(pl.multiple_of(t * PROJ, PROJ), PROJ)

        @pl.loop(0, 2048 // ROWS)
        def _(i):
            rows = pl.ds(pl.multiple_of(i * ROWS, ROWS), ROWS)
            proj = gbuf[rows, cols].astype(F32) - dot(x4[rows, :], c4[...])
            gbuf[rows, cols] = proj.astype(BF16)
            psq[rows, cols] = (proj * proj).astype(BF16)

    def send_sums():
        pack()
        each(nz, zpeer, lambda j: h_copy(j).start())

    def total_sums():
        each(nz, zpeer, lambda j: h_from(j).wait_recv())
        hr[z] = hs[z]
        total = hr[0]
        for j in range(1, nz):
            total = total + hr[j]
        return total

    def share(delta):
        bcur[0:1, :] = bcur[0:1, :] + delta
        br[z] = bcur[...]
        each(nz, zpeer, lambda j: b_copy(j).start())

    def collect():
        each(nz, zpeer, lambda j: b_from(j).wait_recv())
        rows = br[:, 0, :]
        bet[...] = jnp.concatenate([rows, pltpu.roll(rows, 64, 1)], axis=0)
        each(nz, zpeer, lambda j: h_copy(j).wait_send())

    gcopy.wait()
    crosses()
    upright()
    x_from(2).wait_recv()
    x_relay().start()
    x_from(1).wait_recv()
    split(block_at(1))
    split(block_at(2))
    each(4, lambda i: block_at(i), lambda j: p_from(j).wait_recv())
    x_from(3).wait_recv()
    split(block_at(3))
    products()
    send_sums()
    gram = exact_t(xhl[...], xhl[...])
    grs[...] = fold(gram[0:64, :] + gram[64:128, :])
    each(nz, zpeer, lambda j: gr_copy(j).start())
    each(ns, speer, lambda j: c_copy(j).start())
    each(nz, zpeer, lambda j: gr_from(j).wait_recv())
    grr[z] = grs[...]
    gram = grr[0]
    for j in range(1, nz):
        gram = gram + grr[j]
    ginv_ref[...] = sweep(gram, True)
    share(sweep(total_sums(), False))
    collect()

    @pl.loop(1, ITERS)
    def _(it):
        products()
        send_sums()

        @pl.when(it == 1)
        def _():
            each(ns, speer, lambda j: c_from(j).wait_recv())
            crr[s] = crs[s]
            cross = crr[0]
            for j in range(1, ns):
                cross = cross + crr[j]
            hi, lo = two(exact(-ginv_ref[:, 0:64], cross))
            cfall[s, 0:64, :] = hi
            cfall[s, 64:128, :] = lo
            each(ns, speer, lambda j: f_copy(j).start())
            each(nv, vpeer, lambda j: y_copy(j).start())

        @pl.when(it == 2)
        def _():
            each(ns, speer, lambda j: f_from(j).wait_recv())

        @pl.when(it >= 2)
        def _():
            @pl.loop((it - 2) * 4, (it - 1) * 4)
            def _(t):
                project(t)

        delta = sweep(total_sums(), False)
        each(nz, zpeer, lambda j: b_copy(j).wait_send())
        share(delta)
        collect()

    ball[place] = bet[...]
    each(plane, ppeer, lambda j: v_copy(j).start())
    each(nv, vpeer, lambda j: y_from(j).wait_recv())
    yall[v] = ybuf[...]
    each(plane, ppeer, lambda j: v_from(j).wait_recv())

    @pl.loop(0, nv)
    def _(u):
        rows = ball[pl.ds(u * 4, 4)].reshape(32, 128)
        eta = exact(rows[:, 0:64], xt_ref[...])
        fitted = 1.0 / (1.0 + jnp.exp(-eta))
        coded = yall[u]
        seen = coded >= 0.0
        resid = jnp.where(seen, coded - fitted, 0.0).astype(BF16)
        wslab = jnp.where(seen, fitted * (1.0 - fitted), 0.0).astype(BF16)
        wide = resid.astype(F32)
        square = (wide * wide).astype(BF16)
        for h in range(2):
            half = slice(h * 16, (h + 1) * 16)
            at = pl.multiple_of(u * 16 + h * 128, 16)
            r1[pl.ds(at, 16), :] = resid[half]
            r2[pl.ds(at, 16), :] = square[half]
            r2[pl.ds(at + 256, 16), :] = wslab[half]

    width = 2048 // TILES

    def a_copy(t):
        return remote(asd.at[t], arv.at[t], a_ss.at[t], a_rs.at[t], s + 1 - 2 * core, v)

    def q_copy(t, q):
        return remote(bsd.at[t, q], brv.at[t, myq], q_ss.at[t, q], q_rs.at[t, myq], 2 * q + core, v)

    def q_from(t, q):
        return remote(bsd.at[t, q], brv.at[t, q], q_ss.at[t, q], q_rs.at[t, q], 2 * q + core, v)

    def others(do):
        @pl.loop(1, ns // 2)
        def _(d):
            do(lax.rem(myq + d, ns // 2))

    @pl.loop(0, TILES + 1)
    def _(t):
        @pl.when(t < TILES)
        def _():
            slot = lax.rem(t, 2)
            cols = pl.ds(pl.multiple_of(t * width, width), width)
            so[slot, 0:256, :] = dot(r1[...], gbuf[:, cols])
            so[slot, 256:768, :] = dot(r2[...], psq[:, cols])

            @pl.loop(0, ns // 2)
            def _(q):
                at = pl.multiple_of((1 - core) * 128 + q * 16, 16)
                hi, lo = two(so[slot, pl.ds(at, 16), :])
                asd[t, q, 0:16, :] = hi
                asd[t, q, 16:32, :] = lo
                asd[t, q, 32:48, :] = so[slot, pl.ds(at + 256, 16), :].astype(BF16)
                asd[t, q, 48:64, :] = so[slot, pl.ds(at + 512, 16), :].astype(BF16)

            a_copy(t).start()

        @pl.when(t > 0)
        def _():
            b = t - 1
            slot = lax.rem(b, 2)
            a_copy(b).wait_recv()

            def total(q):
                at = pl.multiple_of(core * 128 + q * 16, 16)
                score = so[slot, pl.ds(at, 16), :]
                score = score + arv[b, q, 0:16, :].astype(F32) + arv[b, q, 16:32, :].astype(F32)
                robust = so[slot, pl.ds(at + 256, 16), :] + arv[b, q, 32:48, :].astype(F32)
                model = so[slot, pl.ds(at + 512, 16), :] + arv[b, q, 48:64, :].astype(F32)
                return score, robust, model

            def send(q):
                score, robust, model = total(q)
                hi, lo = two(score)
                bsd[b, q, 0:16, :] = hi
                bsd[b, q, 16:32, :] = lo
                bsd[b, q, 32:48, :] = robust.astype(BF16)
                bsd[b, q, 48:64, :] = model.astype(BF16)
                q_copy(b, q).start()

            others(send)
            score, robust, model = total(myq)
            fin[b, 0:16, :] = score
            fin[b, 16:32, :] = robust
            fin[b, 32:48, :] = model

    for t in range(TILES):
        others(lambda q: q_from(t, q).wait_recv())
        brv[t, myq] = jnp.zeros((64, width), BF16)
        score, robust, model = fin[t, 0:16, :], fin[t, 16:32, :], fin[t, 32:48, :]
        for q in range(ns // 2):
            score = score + brv[t, q, 0:16, :].astype(F32) + brv[t, q, 16:32, :].astype(F32)
            robust = robust + brv[t, q, 32:48, :].astype(F32)
            model = model + brv[t, q, 48:64, :].astype(F32)
        cols = slice(t * width, (t + 1) * width)
        tot_ref[0:16, cols] = score
        tot_ref[16:32, cols] = robust
        tot_ref[32:48, cols] = model

    x_across().wait_send()
    x_beside().wait_send()
    x_relay().wait_send()
    each(4, lambda i: block_at(i), lambda j: p_copy(j).wait_send())
    each(nz, zpeer, lambda j: b_copy(j).wait_send())
    each(nz, zpeer, lambda j: gr_copy(j).wait_send())
    each(ns, speer, lambda j: c_copy(j).wait_send())
    each(ns, speer, lambda j: f_copy(j).wait_send())
    each(nv, vpeer, lambda j: y_copy(j).wait_send())
    each(plane, ppeer, lambda j: v_copy(j).wait_send())

    @pl.loop(0, TILES)
    def _(t):
        a_copy(t).wait_send()
        others(lambda q: q_copy(t, q).wait_send())


def per_device(ns, nv, genotype, covariates, outcome, cohort, measured):
    vm = pltpu.VMEM
    dma = pltpu.SemaphoreType.DMA
    width = 2048 // TILES
    nz = ns // 4
    scratch = [
        vm((2048, 2048), BF16),
        vm((2048, 2048), BF16),
        vm((64, 8192), F32),
        vm((128, 8192), BF16),
        vm((2048, 256), BF16),
        vm((32, 2048), F32),
        vm((8, 8192), F32),
        vm((nv, 32, 2048), F32),
        vm((8, 8192), F32),
        vm((544, 8192), BF16),
        vm((544, 128), F32),
        vm((nz, 72, 128), F32),
        vm((nz, 72, 128), F32),
        vm((ns, 64, 128), F32),
        vm((ns, 64, 128), F32),
        vm((64, 128), F32),
        vm((nz, 64, 128), F32),
        vm((64, 128), F32),
        vm((8, 128), F32),
        vm((nz, 8, 128), F32),
        vm((8, 128), F32),
        vm((4 * nv, 8, 128), F32),
        vm((256, PROJ), BF16),
        vm((ns, 128, 128), BF16),
        vm((256, 2048), BF16),
        vm((512, 2048), BF16),
        vm((2, 768, width), F32),
        vm((TILES, ns // 2, 64, width), BF16),
        vm((TILES, ns // 2, 64, width), BF16),
        vm((TILES, ns // 2, 64, width), BF16),
        vm((TILES, ns // 2, 64, width), BF16),
        vm((TILES, 48, width), F32),
        dma,
    ]
    scratch += [dma((ns,))] * 4 + [dma((nz,))] * 6 + [dma((4,))] * 4 + [dma((nv,))] * 2
    scratch += [dma((4 * nv,))] * 2 + [dma((TILES,))] * 2 + [dma((TILES, ns // 2))] * 2
    inside = pl.BlockSpec(memory_space=pltpu.VMEM)
    totals = pl.pallas_call(
        functools.partial(kernel, ns, nv),
        out_shape=jax.ShapeDtypeStruct((48, 2048), F32),
        in_specs=[pl.BlockSpec(memory_space=pl.ANY)] + [inside] * 4,
        out_specs=inside,
        scratch_shapes=scratch,
        compiler_params=pltpu.CompilerParams(
            collective_id=0, has_side_effects=True, vmem_limit_bytes=60 * 2**20
        ),
        name="score_tests",
    )(genotype, covariates.T, outcome.T, cohort[None, :], measured.T)
    score, robust, model = totals[0:16], totals[16:32], totals[32:48]
    return score * lax.rsqrt(robust + EPS), score * lax.rsqrt(model + EPS)


def solution(mesh):
    placed = (
        P("sample", "variant"),
        P("sample", None),
        P("sample", "variant"),
        P("sample"),
        P("variant", None),
    )
    return jax.shard_map(
        functools.partial(per_device, mesh.shape["sample"], mesh.shape["variant"]),
        mesh=mesh,
        in_specs=placed,
        out_specs=(P("sample", "variant"), P("sample", "variant")),
        check_vma=False,
    )
```

```python
import functools

import jax
import jax.numpy as jnp
from jax import lax
from jax.experimental import pallas as pl
from jax.experimental.pallas import tpu as pltpu
from jax.sharding import PartitionSpec as P

ITERS = 4
EPS = 1e-06
HIGHEST = lax.Precision.HIGHEST
F32 = jnp.float32
BF16 = jnp.bfloat16
TILES = 4
PROJ = 256
ROWS = 512


def dot(a, b):
    return jnp.dot(a, b, preferred_element_type=F32)


def exact(a, b):
    return jnp.dot(a, b, preferred_element_type=F32, precision=HIGHEST)


def two(x):
    hi = x.astype(BF16)
    return hi, (x - hi.astype(F32)).astype(BF16)


def fold(x):
    return x + pltpu.roll(x, 64, 1)


def exact_t(a, b):
    return lax.dot_general(a, b, (((1,), (1,)), ((), ())), preferred_element_type=F32)


def product(x, y):
    out = []
    for i in range(len(x)):
        line = []
        for j in range(len(y[0])):
            term = x[i][0] * y[0][j]
            for k in range(1, len(y)):
                term = term + x[i][k] * y[k][j]
            line.append(term)
        out.append(line)
    return out


def inverse2(a):
    (p, q), (_, d) = a
    i = 1.0 / (p * d - q * q)
    return [[d * i, -(q * i)], [-(q * i), p * i]]


def inverse4(a):
    right = [r[2:] for r in a[:2]]
    corner = [r[2:] for r in a[2:]]
    flip = lambda x: [list(c) for c in zip(*x)]
    first = inverse2([r[:2] for r in a[:2]])
    lead = product(first, right)
    inner = product(flip(right), lead)
    last = inverse2([[corner[i][j] - inner[i][j] for j in range(2)] for i in range(2)])
    side = product(lead, last)
    more = product(side, flip(lead))
    top = [[first[i][j] + more[i][j] for j in range(2)] + [-side[i][j] for j in range(2)] for i in range(2)]
    return top + [[-side[j][i] for j in range(2)] + last[i] for i in range(2)]


def sweep(m, full):
    lane = lax.broadcasted_iota(jnp.int32, (1, 128), 1)
    low = lane < 64
    place = jnp.where(low, lane, lane - 64)
    height = lax.broadcasted_iota(jnp.int32, (64, 1), 0)
    for k in range(0, 64, 4):
        if not full and k % 8 == 0 and k:
            m = m[8:, :]
        r = k if full else k % 8
        cols = [jnp.where(low, m[:, k + j : k + j + 1], m[:, 64 + k + j : 65 + k + j]) for j in range(4)]
        pivot = [[cols[max(i, j)][r + min(i, j) : r + min(i, j) + 1, :] for j in range(4)] for i in range(4)]
        here = (place >= k) & (place < k + 4)
        lines = [
            [jnp.where(here, jnp.where(place == k + j, -1.0, 0.0), m[r + j : r + j + 1, :])] for j in range(4)
        ]
        lines = product(inverse4(pivot), lines)
        m = jnp.where(here, 0.0, m)
        if full:
            mine = (height >= k) & (height < k + 4)
            m = jnp.where(mine, 0.0, m)
            cols = [jnp.where(mine, jnp.where(height == k + j, -1.0, 0.0), cols[j]) for j in range(4)]
        m = m - product([cols], lines)[0][0]
    return m if full else m[8:9, :]


def kernel(
    ns,
    nv,
    g_hbm,
    xt_ref,
    out_ref,
    cohort_ref,
    meas_ref,
    tot_ref,
    gbuf,
    psq,
    xt4,
    xhl,
    x4,
    ybuf,
    y4,
    yall,
    wbuf,
    lhs,
    hacc,
    hs,
    hr,
    crs,
    crr,
    grs,
    grr,
    ginv_ref,
    bcur,
    br,
    bet,
    ball,
    c4,
    cfall,
    r1,
    r2,
    so,
    asd,
    arv,
    bsd,
    brv,
    fin,
    g_sem,
    c_ss,
    c_rs,
    f_ss,
    f_rs,
    h_ss,
    h_rs,
    gr_ss,
    gr_rs,
    b_ss,
    b_rs,
    x_ss,
    x_rs,
    l_ss,
    l_rs,
    p_ss,
    p_rs,
    y_ss,
    y_rs,
    v_ss,
    v_rs,
    a_ss,
    a_rs,
    q_ss,
    q_rs,
    told,
):
    nz = ns // 4
    s = lax.axis_index("sample")
    v = lax.axis_index("variant")
    z = s // 4
    sub = lax.rem(s, 4)
    core = lax.rem(s, 2)
    xh = sub // 2
    myq = s // 2
    sibling = s + 1 - 2 * core
    across = s + 2 - 4 * xh
    near = v + 1 - 2 * lax.rem(v, 2)
    low = lax.broadcasted_iota(jnp.int32, (1, 128), 1) < 64
    mesh_id = pl.DeviceIdType.MESH

    gcopy = pltpu.make_async_copy(g_hbm, gbuf, g_sem)
    gcopy.start()

    def block(b):
        return pl.ds(pl.multiple_of(b * 2048, 2048), 2048)

    def split(b):
        hi, lo = two(xt4[:, block(b)])
        xhl[0:64, block(b)] = hi
        xhl[64:128, block(b)] = lo

    def join(b):
        xt4[:, block(b)] = xhl[0:64, block(b)].astype(F32) + xhl[64:128, block(b)].astype(F32)

    def block_at(i):
        return 2 * lax.rem(xh + i // 2, 2) + lax.rem(core + i, 2)

    def speer(d):
        return lax.rem(s + d, ns)

    def zpeer(d):
        return lax.rem(z + d, nz)

    def vpeer(d):
        return lax.rem(v + d, nv)

    def remote(src, dst, ss, rs, sample, variant):
        return pltpu.make_async_remote_copy(
            src_ref=src,
            dst_ref=dst,
            send_sem=ss,
            recv_sem=rs,
            device_id=(sample, variant),
            device_id_type=mesh_id,
        )

    def each(n, peer, do):
        @pl.loop(1, n)
        def _(d):
            do(peer(d))

    barrier = pltpu.get_barrier_semaphore()

    def greet(sample, variant):
        pl.semaphore_signal(barrier, inc=1, device_id=(sample, variant), device_id_type=mesh_id)

    plane = 4 * nv
    place = v * 4 + sub

    def ppeer(d):
        return lax.rem(place + d, plane)

    greet(across, near)
    for d in (1, 2, 3):
        greet(4 * z + lax.rem(sub + d, 4), v)
    for d in (2, 1, 3):
        greet(4 * zpeer(d) + sub, v)
    for d in range(2, nv, 2):
        greet(s, vpeer(d))

    hot = lax.broadcasted_iota(jnp.int32, (16, 2048), 0) == cohort_ref[...]
    mask = lax.dot_general(
        meas_ref[...].astype(BF16),
        hot.astype(BF16),
        (((0,), (0,)), ((), ())),
        preferred_element_type=F32,
    )
    ybuf[...] = jnp.where(mask > 0.5, out_ref[...], -1.0)
    own = block(sub)
    y4[:, own] = ybuf[pl.ds(pl.multiple_of(sub * 8, 8), 8), :]
    xt4[:, own] = xt_ref[...]
    split(sub)
    bcur[...] = jnp.zeros_like(bcur)
    br[...] = jnp.zeros_like(br)
    bet[...] = jnp.zeros_like(bet)
    hs[...] = jnp.zeros_like(hs)

    pl.semaphore_wait(barrier, 7 + nv // 2 - 1)

    def part(low_part, b):
        return xhl.at[pl.ds(64 * low_part, 64), block(b)]

    def x_sems(low_part, i):
        return (l_ss.at[i], l_rs.at[i]) if low_part else (x_ss.at[i], x_rs.at[i])

    def x_beside(low_part):
        mine = part(low_part, sub)
        return remote(mine, mine, *x_sems(low_part, 1), sibling, v)

    def x_across(low_part):
        mine = part(low_part, sub)
        return remote(mine, mine, *x_sems(low_part, 2), across, near)

    def x_relay(low_part):
        theirs = part(low_part, block_at(2))
        return remote(theirs, theirs, *x_sems(low_part, 3), sibling, v)

    def x_from(low_part, i):
        theirs = part(low_part, block_at(i))
        return remote(theirs, theirs, *x_sems(low_part, i), sibling, v)

    def p_copy(j):
        rows = pl.ds(pl.multiple_of(j * 8, 8), 8)
        return remote(ybuf.at[rows], y4.at[:, own], p_ss.at[j], p_rs.at[sub], 4 * z + j, v)

    def p_from(j):
        rows = pl.ds(pl.multiple_of(j * 8, 8), 8)
        return remote(ybuf.at[rows], y4.at[:, block(j)], p_ss.at[j], p_rs.at[j], 4 * z + j, v)

    def y_copy(j):
        return remote(ybuf, yall.at[v], y_ss.at[j], y_rs.at[v], s, j)

    def y_from(j):
        return remote(ybuf, yall.at[j], y_ss.at[j], y_rs.at[j], s, j)

    def gr_copy(j):
        return remote(grs, grr.at[z], gr_ss.at[j], gr_rs.at[z], 4 * j + sub, v)

    def gr_from(j):
        return remote(grs, grr.at[j], gr_ss.at[j], gr_rs.at[j], 4 * j + sub, v)

    def h_copy(j):
        return remote(hs.at[j], hr.at[z], h_ss.at[j], h_rs.at[z], 4 * j + sub, v)

    def h_from(j):
        return remote(hs.at[j], hr.at[j], h_ss.at[j], h_rs.at[j], 4 * j + sub, v)

    def b_copy(j):
        return remote(br.at[z], br.at[z], b_ss.at[j], b_rs.at[z], 4 * j + sub, v)

    def b_from(j):
        return remote(br.at[z], br.at[j], b_ss.at[j], b_rs.at[j], 4 * j + sub, v)

    def c_copy(j):
        return remote(crs.at[j], crr.at[s], c_ss.at[j], c_rs.at[s], j, v)

    def c_from(j):
        return remote(crs.at[j], crr.at[j], c_ss.at[j], c_rs.at[j], j, v)

    def f_copy(j):
        return remote(cfall.at[s], cfall.at[s], f_ss.at[j], f_rs.at[s], j, v)

    def f_from(j):
        return remote(cfall.at[s], cfall.at[j], f_ss.at[j], f_rs.at[j], j, v)

    def v_copy(j):
        to = 4 * z + lax.rem(j, 4)
        mine = ball.at[place]
        return remote(mine, mine, v_ss.at[j], v_rs.at[place], to, j // 4)

    def v_from(j):
        to = 4 * z + lax.rem(j, 4)
        return remote(ball.at[place], ball.at[j], v_ss.at[j], v_rs.at[j], to, j // 4)

    x_across(0).start()
    x_beside(0).start()
    each(4, lambda i: block_at(i), lambda j: p_copy(j).start())

    def products():
        beta = bet[:, 0:64]
        b_hi = beta.astype(BF16).astype(F32)
        rest = beta - b_hi
        b_mid = rest.astype(BF16).astype(F32)
        none = jnp.zeros_like(beta)
        rows = jnp.concatenate([b_hi, b_mid, rest - b_mid, none], axis=0)
        rows = jnp.concatenate([rows, rows], axis=1).astype(BF16)
        eta = dot(rows, xhl[...])
        eta = eta[0:8] + eta[8:16] + eta[16:24]
        fitted = 1.0 / (1.0 + jnp.exp(-eta))
        coded = y4[...]
        seen = coded >= 0.0
        wbuf[...] = jnp.where(seen, fitted * (1.0 - fitted), 0.0)
        work = jnp.where(seen, coded - fitted, 0.0)
        r_hi = work.astype(BF16).astype(F32)
        rest = work - r_hi
        r_mid = rest.astype(BF16).astype(F32)
        none = jnp.zeros_like(work)
        lhs[512:544, :] = jnp.concatenate([r_hi, r_mid, rest - r_mid, none], axis=0).astype(BF16)

        @pl.loop(0, 16)
        def _(i):
            cols = pl.ds(pl.multiple_of(i * 512, 512), 512)
            table = xt4[:, cols]
            for p in range(8):
                lhs[p * 64 : (p + 1) * 64, cols] = (table * wbuf[p : p + 1, cols]).astype(BF16)

        hacc[...] = fold(exact_t(lhs[...], xhl[...]))

    def products0():
        coded = y4[...]
        seen = coded >= 0.0
        wbuf[...] = jnp.where(seen, 0.25, 0.0)
        work = jnp.where(seen, coded - 0.5, 0.0)
        r_hi = work.astype(BF16).astype(F32)
        rest = work - r_hi
        r_mid = rest.astype(BF16).astype(F32)
        none = jnp.zeros_like(work)
        lhs[512:544, :] = jnp.concatenate([r_hi, r_mid, rest - r_mid, none], axis=0).astype(BF16)

        @pl.loop(0, 16)
        def _(i):
            cols = pl.ds(pl.multiple_of(i * 512, 512), 512)
            table = xhl[0:64, cols].astype(F32)
            for p in range(8):
                lhs[p * 64 : (p + 1) * 64, cols] = (table * wbuf[p : p + 1, cols]).astype(BF16)

        out = exact_t(lhs[...], xhl[0:64, :])
        hacc[...] = jnp.concatenate([out, out], axis=1)

    def send_sums():
        grads = hacc[512:520, :] + hacc[520:528, :] + hacc[528:536, :]
        line = lax.broadcasted_iota(jnp.int32, (4, 1), 0)

        def one(j):
            first = hacc[pl.ds(pl.multiple_of(j * 64, 64), 64), :]
            second = hacc[pl.ds(pl.multiple_of((j + nz) * 64, 64), 64), :]
            hs[j, 0:64, :] = jnp.where(low, first, second)
            pair = jnp.where(low, grads[0:4], grads[4:8])
            hs[j, 64:65, :] = jnp.sum(jnp.where(line == j, pair, 0.0), axis=0, keepdims=True)

        for d in (2, 1, 3):
            one(zpeer(d))
            h_copy(zpeer(d)).start()
        one(z)

    def crosses():
        @pl.loop(0, 8)
        def _(t):
            out = dot(xhl[:, own], gbuf[:, pl.ds(pl.multiple_of(t * 256, 256), 256)])
            out = out[0:64] + out[64:128]
            crs[2 * t] = out[:, 0:128]
            crs[2 * t + 1] = out[:, 128:256]

    def upright():
        @pl.loop(0, 16)
        def _(i):
            at = pl.ds(pl.multiple_of(i * 128, 128), 128)
            from_ = pl.ds(pl.multiple_of(sub * 2048 + i * 128, 128), 128)
            both = xhl[:, from_].astype(F32).T.astype(BF16)
            x4[at, 0:128] = both
            x4[at, 128:256] = both

    def project(t):
        for h in range(2):
            part = cfall[2 * t + h]
            cols = slice(h * 128, (h + 1) * 128)
            c4[0:64, cols] = part[0:64]
            c4[64:128, cols] = part[0:64]
            c4[128:192, cols] = part[64:128]
            c4[192:256, cols] = part[64:128]
        cols = pl.ds(pl.multiple_of(t * PROJ, PROJ), PROJ)

        @pl.loop(0, 2048 // ROWS)
        def _(i):
            rows = pl.ds(pl.multiple_of(i * ROWS, ROWS), ROWS)
            proj = gbuf[rows, cols].astype(F32) - dot(x4[rows, :], c4[...])
            gbuf[rows, cols] = proj.astype(BF16)
            psq[rows, cols] = (proj * proj).astype(BF16)

    def total_sums():
        total = hs[z]
        for d in (1, 3, 2):
            h_from(zpeer(d)).wait_recv()
            total = total + hr[zpeer(d)]
        return total

    def share(delta):
        bcur[0:1, :] = bcur[0:1, :] + delta
        br[z] = bcur[...]
        for d in (2, 1, 3):
            b_copy(zpeer(d)).start()

    def collect():
        for d in (1, 3, 2):
            b_from(zpeer(d)).wait_recv()
        rows = br[:, 0, :]
        bet[...] = jnp.concatenate([rows, pltpu.roll(rows, 64, 1)], axis=0)
        for d in (1, 2, 3):
            h_copy(zpeer(d)).wait_send()

    gcopy.wait()
    crosses()
    x_from(0, 2).wait_recv()
    x_relay(0).start()
    for d in (1, 2, 3):
        pl.semaphore_signal(
            told, inc=1, device_id=(4 * z + lax.rem(sub + d, 4), v), device_id_type=mesh_id
        )
    x_across(1).start()
    x_beside(1).start()
    upright()
    x_from(0, 1).wait_recv()
    each(4, lambda i: block_at(i), lambda j: p_from(j).wait_recv())
    x_from(0, 3).wait_recv()
    products0()
    send_sums()
    x_from(1, 2).wait_recv()
    x_relay(1).start()
    join(block_at(2))
    x_from(1, 1).wait_recv()
    join(block_at(1))
    x_from(1, 3).wait_recv()
    join(block_at(3))
    pl.semaphore_wait(told, 3)
    share(sweep(total_sums(), False))
    gram = exact_t(xhl[...], xhl[...])
    grs[...] = fold(gram[0:64, :] + gram[64:128, :])
    for d in (2, 1, 3):
        gr_copy(zpeer(d)).start()
    collect()
    each(ns, speer, lambda j: c_copy(j).start())

    @pl.loop(1, ITERS)
    def _(it):
        products()
        send_sums()

        @pl.when(it == 1)
        def _():
            gram = grs[...]
            for d in (1, 3, 2):
                gr_from(zpeer(d)).wait_recv()
                gram = gram + grr[zpeer(d)]
            ginv_ref[...] = sweep(gram, True)

        @pl.when(it == 2)
        def _():
            each(ns, speer, lambda j: f_from(j).wait_recv())

        @pl.when(it >= 2)
        def _():
            @pl.loop((it - 2) * 4, (it - 2) * 4 + 2)
            def _(t):
                project(t)

        delta = sweep(total_sums(), False)
        each(nz, zpeer, lambda j: b_copy(j).wait_send())
        share(delta)

        @pl.when(it == 1)
        def _():
            each(ns, speer, lambda j: c_from(j).wait_recv())
            crr[s] = crs[s]
            cross = crr[0]
            for j in range(1, ns):
                cross = cross + crr[j]
            hi, lo = two(exact(-ginv_ref[:, 0:64], cross))
            cfall[s, 0:64, :] = hi
            cfall[s, 64:128, :] = lo
            each(ns, speer, lambda j: f_copy(j).start())
            each(nv, vpeer, lambda j: y_copy(j).start())

        @pl.when(it >= 2)
        def _():
            @pl.loop((it - 2) * 4 + 2, (it - 1) * 4)
            def _(t):
                project(t)

        collect()

    ball[place] = bet[...]
    each(plane, ppeer, lambda j: v_copy(j).start())
    each(nv, vpeer, lambda j: y_from(j).wait_recv())
    yall[v] = ybuf[...]
    each(plane, ppeer, lambda j: v_from(j).wait_recv())

    @pl.loop(0, nv)
    def _(u):
        rows = ball[pl.ds(u * 4, 4)].reshape(32, 128)
        eta = exact(rows[:, 0:64], xt_ref[...])
        fitted = 1.0 / (1.0 + jnp.exp(-eta))
        coded = yall[u]
        seen = coded >= 0.0
        resid = jnp.where(seen, coded - fitted, 0.0).astype(BF16)
        wslab = jnp.where(seen, fitted * (1.0 - fitted), 0.0).astype(BF16)
        wide = resid.astype(F32)
        square = (wide * wide).astype(BF16)
        for h in range(2):
            half = slice(h * 16, (h + 1) * 16)
            at = pl.multiple_of(u * 16 + h * 128, 16)
            r1[pl.ds(at, 16), :] = resid[half]
            r2[pl.ds(at, 16), :] = square[half]
            r2[pl.ds(at + 256, 16), :] = wslab[half]

    width = 2048 // TILES

    def a_copy(t):
        return remote(asd.at[t], arv.at[t], a_ss.at[t], a_rs.at[t], s + 1 - 2 * core, v)

    def q_copy(t, q):
        return remote(bsd.at[t, q], brv.at[t, myq], q_ss.at[t, q], q_rs.at[t, myq], 2 * q + core, v)

    def q_from(t, q):
        return remote(bsd.at[t, q], brv.at[t, q], q_ss.at[t, q], q_rs.at[t, q], 2 * q + core, v)

    def others(do):
        @pl.loop(1, ns // 2)
        def _(d):
            do(lax.rem(myq + d, ns // 2))

    @pl.loop(0, TILES + 1)
    def _(t):
        @pl.when(t < TILES)
        def _():
            slot = lax.rem(t, 2)
            cols = pl.ds(pl.multiple_of(t * width, width), width)
            so[slot, 0:256, :] = dot(r1[...], gbuf[:, cols])
            so[slot, 256:768, :] = dot(r2[...], psq[:, cols])

            @pl.loop(0, ns // 2)
            def _(q):
                at = pl.multiple_of((1 - core) * 128 + q * 16, 16)
                hi, lo = two(so[slot, pl.ds(at, 16), :])
                asd[t, q, 0:16, :] = hi
                asd[t, q, 16:32, :] = lo
                asd[t, q, 32:48, :] = so[slot, pl.ds(at + 256, 16), :].astype(BF16)
                asd[t, q, 48:64, :] = so[slot, pl.ds(at + 512, 16), :].astype(BF16)

            a_copy(t).start()

        @pl.when(t > 0)
        def _():
            b = t - 1
            slot = lax.rem(b, 2)
            a_copy(b).wait_recv()

            def total(q):
                at = pl.multiple_of(core * 128 + q * 16, 16)
                score = so[slot, pl.ds(at, 16), :]
                score = score + arv[b, q, 0:16, :].astype(F32) + arv[b, q, 16:32, :].astype(F32)
                robust = so[slot, pl.ds(at + 256, 16), :] + arv[b, q, 32:48, :].astype(F32)
                model = so[slot, pl.ds(at + 512, 16), :] + arv[b, q, 48:64, :].astype(F32)
                return score, robust, model

            def send(q):
                score, robust, model = total(q)
                bsd[b, q, 0:16, :] = score.astype(BF16)
                bsd[b, q, 16:32, :] = robust.astype(BF16)
                bsd[b, q, 32:48, :] = model.astype(BF16)
                q_copy(b, q).start()

            others(send)
            score, robust, model = total(myq)
            fin[b, 0:16, :] = score
            fin[b, 16:32, :] = robust
            fin[b, 32:48, :] = model

    for low_part in range(2):
        x_across(low_part).wait_send()
        x_beside(low_part).wait_send()
        x_relay(low_part).wait_send()
    each(4, lambda i: block_at(i), lambda j: p_copy(j).wait_send())
    each(nz, zpeer, lambda j: b_copy(j).wait_send())
    each(nz, zpeer, lambda j: gr_copy(j).wait_send())
    each(ns, speer, lambda j: c_copy(j).wait_send())
    each(ns, speer, lambda j: f_copy(j).wait_send())
    each(nv, vpeer, lambda j: y_copy(j).wait_send())
    each(plane, ppeer, lambda j: v_copy(j).wait_send())

    for t in range(TILES):
        others(lambda q: q_from(t, q).wait_recv())
        brv[t, myq] = jnp.zeros((48, width), BF16)
        score, robust, model = fin[t, 0:16, :], fin[t, 16:32, :], fin[t, 32:48, :]
        for q in range(ns // 2):
            score = score + brv[t, q, 0:16, :].astype(F32)
            robust = robust + brv[t, q, 16:32, :].astype(F32)
            model = model + brv[t, q, 32:48, :].astype(F32)
        cols = slice(t * width, (t + 1) * width)
        tot_ref[0:16, cols] = score
        tot_ref[16:32, cols] = robust
        tot_ref[32:48, cols] = model

    @pl.loop(0, TILES)
    def _(t):
        a_copy(t).wait_send()
        others(lambda q: q_copy(t, q).wait_send())


def per_device(ns, nv, genotype, covariates, outcome, cohort, measured):
    vm = pltpu.VMEM
    dma = pltpu.SemaphoreType.DMA
    width = 2048 // TILES
    nz = ns // 4
    scratch = [
        vm((2048, 2048), BF16),
        vm((2048, 2048), BF16),
        vm((64, 8192), F32),
        vm((128, 8192), BF16),
        vm((2048, 256), BF16),
        vm((32, 2048), F32),
        vm((8, 8192), F32),
        vm((nv, 32, 2048), F32),
        vm((8, 8192), F32),
        vm((544, 8192), BF16),
        vm((544, 128), F32),
        vm((nz, 72, 128), F32),
        vm((nz, 72, 128), F32),
        vm((ns, 64, 128), F32),
        vm((ns, 64, 128), F32),
        vm((64, 128), F32),
        vm((nz, 64, 128), F32),
        vm((64, 128), F32),
        vm((8, 128), F32),
        vm((nz, 8, 128), F32),
        vm((8, 128), F32),
        vm((4 * nv, 8, 128), F32),
        vm((256, PROJ), BF16),
        vm((ns, 128, 128), BF16),
        vm((256, 2048), BF16),
        vm((512, 2048), BF16),
        vm((2, 768, width), F32),
        vm((TILES, ns // 2, 64, width), BF16),
        vm((TILES, ns // 2, 64, width), BF16),
        vm((TILES, ns // 2, 48, width), BF16),
        vm((TILES, ns // 2, 48, width), BF16),
        vm((TILES, 48, width), F32),
        dma,
    ]
    scratch += [dma((ns,))] * 4 + [dma((nz,))] * 6 + [dma((4,))] * 6 + [dma((nv,))] * 2
    scratch += [dma((4 * nv,))] * 2 + [dma((TILES,))] * 2 + [dma((TILES, ns // 2))] * 2
    scratch.append(pltpu.SemaphoreType.REGULAR)
    inside = pl.BlockSpec(memory_space=pltpu.VMEM)
    totals = pl.pallas_call(
        functools.partial(kernel, ns, nv),
        out_shape=jax.ShapeDtypeStruct((48, 2048), F32),
        in_specs=[pl.BlockSpec(memory_space=pl.ANY)] + [inside] * 4,
        out_specs=inside,
        scratch_shapes=scratch,
        compiler_params=pltpu.CompilerParams(
            collective_id=0, has_side_effects=True, vmem_limit_bytes=60 * 2**20
        ),
        name="score_tests",
    )(genotype, covariates.T, outcome.T, cohort[None, :], measured.T)
    score, robust, model = totals[0:16], totals[16:32], totals[32:48]
    return score * lax.rsqrt(robust + EPS), score * lax.rsqrt(model + EPS)


def solution(mesh):
    placed = (
        P("sample", "variant"),
        P("sample", None),
        P("sample", "variant"),
        P("sample"),
        P("variant", None),
    )
    return jax.shard_map(
        functools.partial(per_device, mesh.shape["sample"], mesh.shape["variant"]),
        mesh=mesh,
        in_specs=placed,
        out_specs=(P("sample", "variant"), P("sample", "variant")),
        check_vma=False,
    )
```

```python
import functools

import jax
import jax.numpy as jnp
from jax import lax
from jax.experimental import pallas as pl
from jax.experimental.pallas import tpu as pltpu
from jax.sharding import PartitionSpec as P

ITERS = 4
EPS = 1e-06
HIGHEST = lax.Precision.HIGHEST
F32 = jnp.float32
BF16 = jnp.bfloat16
LAG = 6
TILES = 8
PROJ = 256
ROWS = 512


def dot(a, b):
    return jnp.dot(a, b, preferred_element_type=F32)


def exact(a, b):
    return jnp.dot(a, b, preferred_element_type=F32, precision=HIGHEST)


def two(x):
    hi = x.astype(BF16)
    return hi, (x - hi.astype(F32)).astype(BF16)


def fold(x):
    return x + pltpu.roll(x, 64, 1)


def exact_t(a, b):
    return lax.dot_general(a, b, (((1,), (1,)), ((), ())), preferred_element_type=F32)


def product(x, y):
    out = []
    for i in range(len(x)):
        line = []
        for j in range(len(y[0])):
            term = x[i][0] * y[0][j]
            for k in range(1, len(y)):
                term = term + x[i][k] * y[k][j]
            line.append(term)
        out.append(line)
    return out


def inverse2(a):
    (p, q), (_, d) = a
    i = 1.0 / (p * d - q * q)
    return [[d * i, -(q * i)], [-(q * i), p * i]]


def inverse4(a):
    right = [r[2:] for r in a[:2]]
    corner = [r[2:] for r in a[2:]]
    flip = lambda x: [list(c) for c in zip(*x)]
    first = inverse2([r[:2] for r in a[:2]])
    lead = product(first, right)
    inner = product(flip(right), lead)
    last = inverse2([[corner[i][j] - inner[i][j] for j in range(2)] for i in range(2)])
    side = product(lead, last)
    more = product(side, flip(lead))
    top = [[first[i][j] + more[i][j] for j in range(2)] + [-side[i][j] for j in range(2)] for i in range(2)]
    return top + [[-side[j][i] for j in range(2)] + last[i] for i in range(2)]


def sweep(m, full):
    lane = lax.broadcasted_iota(jnp.int32, (1, 128), 1)
    low = lane < 64
    place = jnp.where(low, lane, lane - 64)
    height = lax.broadcasted_iota(jnp.int32, (64, 1), 0)
    for k in range(0, 64, 4):
        if not full and k % 8 == 0 and k:
            m = m[8:, :]
        r = k if full else k % 8
        cols = [jnp.where(low, m[:, k + j : k + j + 1], m[:, 64 + k + j : 65 + k + j]) for j in range(4)]
        pivot = [[cols[max(i, j)][r + min(i, j) : r + min(i, j) + 1, :] for j in range(4)] for i in range(4)]
        here = (place >= k) & (place < k + 4)
        lines = [
            [jnp.where(here, jnp.where(place == k + j, -1.0, 0.0), m[r + j : r + j + 1, :])] for j in range(4)
        ]
        lines = product(inverse4(pivot), lines)
        m = jnp.where(here, 0.0, m)
        if full:
            mine = (height >= k) & (height < k + 4)
            m = jnp.where(mine, 0.0, m)
            cols = [jnp.where(mine, jnp.where(height == k + j, -1.0, 0.0), cols[j]) for j in range(4)]
        m = m - product([cols], lines)[0][0]
    return m if full else m[8:9, :]


def kernel(
    ns,
    nv,
    g_hbm,
    xt_ref,
    out_ref,
    cohort_ref,
    meas_ref,
    tot_ref,
    gbuf,
    psq,
    xt4,
    xhl,
    x4,
    ybuf,
    y4,
    yall,
    wbuf,
    lhs,
    hacc,
    hs,
    hr,
    crs,
    crr,
    cmid,
    crt,
    grs,
    grr,
    ginv_ref,
    bcur,
    br,
    bet,
    ball,
    c4,
    cfall,
    r1,
    r2,
    so,
    asd,
    arv,
    bsd,
    brv,
    keep,
    lsd,
    lrv,
    fin,
    g_sem,
    c_ss,
    c_rs,
    f_ss,
    f_rs,
    h_ss,
    h_rs,
    gr_ss,
    gr_rs,
    b_ss,
    b_rs,
    x_ss,
    x_rs,
    l_ss,
    l_rs,
    p_ss,
    p_rs,
    y_ss,
    y_rs,
    v_ss,
    v_rs,
    a_ss,
    a_rs,
    q_ss,
    q_rs,
    w_ss,
    w_rs,
    told,
):
    nz = ns // 4
    s = lax.axis_index("sample")
    v = lax.axis_index("variant")
    z = s // 4
    sub = lax.rem(s, 4)
    core = lax.rem(s, 2)
    xh = sub // 2
    sibling = s + 1 - 2 * core
    across = s + 2 - 4 * xh
    near = v + 1 - 2 * lax.rem(v, 2)
    low = lax.broadcasted_iota(jnp.int32, (1, 128), 1) < 64
    mesh_id = pl.DeviceIdType.MESH

    gcopy = pltpu.make_async_copy(g_hbm, gbuf, g_sem)
    gcopy.start()

    def block(b):
        return pl.ds(pl.multiple_of(b * 2048, 2048), 2048)

    def split(b):
        hi, lo = two(xt4[:, block(b)])
        xhl[0:64, block(b)] = hi
        xhl[64:128, block(b)] = lo

    def join(b):
        xt4[:, block(b)] = xhl[0:64, block(b)].astype(F32) + xhl[64:128, block(b)].astype(F32)

    def block_at(i):
        return 2 * lax.rem(xh + i // 2, 2) + lax.rem(core + i, 2)

    def zpeer(d):
        return lax.rem(z + d, nz)

    def vpeer(d):
        return lax.rem(v + d, nv)

    def remote(src, dst, ss, rs, sample, variant):
        return pltpu.make_async_remote_copy(
            src_ref=src,
            dst_ref=dst,
            send_sem=ss,
            recv_sem=rs,
            device_id=(sample, variant),
            device_id_type=mesh_id,
        )

    def each(n, peer, do):
        @pl.loop(1, n)
        def _(d):
            do(peer(d))

    barrier = pltpu.get_barrier_semaphore()

    def greet(sample, variant):
        pl.semaphore_signal(barrier, inc=1, device_id=(sample, variant), device_id_type=mesh_id)

    plane = 4 * nv
    place = v * 4 + sub

    def ppeer(d):
        return lax.rem(place + d, plane)

    greet(across, near)
    for d in (1, 2, 3):
        greet(4 * z + lax.rem(sub + d, 4), v)
    for d in (2, 1, 3):
        greet(4 * zpeer(d) + sub, v)
    for d in range(2, nv, 2):
        greet(s, vpeer(d))

    hot = lax.broadcasted_iota(jnp.int32, (16, 2048), 0) == cohort_ref[...]
    mask = lax.dot_general(
        meas_ref[...].astype(BF16),
        hot.astype(BF16),
        (((0,), (0,)), ((), ())),
        preferred_element_type=F32,
    )
    ybuf[...] = jnp.where(mask > 0.5, out_ref[...], -1.0)
    own = block(sub)
    y4[:, own] = ybuf[pl.ds(pl.multiple_of(sub * 8, 8), 8), :]
    xt4[:, own] = xt_ref[...]
    split(sub)
    bcur[...] = jnp.zeros_like(bcur)
    br[...] = jnp.zeros_like(br)
    bet[...] = jnp.zeros_like(bet)
    hs[...] = jnp.zeros_like(hs)

    pl.semaphore_wait(barrier, 7 + nv // 2 - 1)

    def part(low_part, b):
        return xhl.at[pl.ds(64 * low_part, 64), block(b)]

    def x_sems(low_part, i):
        return (l_ss.at[i], l_rs.at[i]) if low_part else (x_ss.at[i], x_rs.at[i])

    def x_beside(low_part):
        mine = part(low_part, sub)
        return remote(mine, mine, *x_sems(low_part, 1), sibling, v)

    def x_across(low_part):
        mine = part(low_part, sub)
        return remote(mine, mine, *x_sems(low_part, 2), across, near)

    def x_relay(low_part):
        theirs = part(low_part, block_at(2))
        return remote(theirs, theirs, *x_sems(low_part, 3), sibling, v)

    def x_from(low_part, i):
        theirs = part(low_part, block_at(i))
        return remote(theirs, theirs, *x_sems(low_part, i), sibling, v)

    def p_copy(j):
        rows = pl.ds(pl.multiple_of(j * 8, 8), 8)
        return remote(ybuf.at[rows], y4.at[:, own], p_ss.at[j], p_rs.at[sub], 4 * z + j, v)

    def p_from(j):
        rows = pl.ds(pl.multiple_of(j * 8, 8), 8)
        return remote(ybuf.at[rows], y4.at[:, block(j)], p_ss.at[j], p_rs.at[j], 4 * z + j, v)

    def y_copy(j):
        return remote(ybuf, yall.at[v], y_ss.at[j], y_rs.at[v], s, j)

    def y_from(j):
        return remote(ybuf, yall.at[j], y_ss.at[j], y_rs.at[j], s, j)

    def gr_copy(j):
        return remote(grs, grr.at[z], gr_ss.at[j], gr_rs.at[z], 4 * j + sub, v)

    def gr_from(j):
        return remote(grs, grr.at[j], gr_ss.at[j], gr_rs.at[j], 4 * j + sub, v)

    def h_copy(j):
        return remote(hs.at[j], hr.at[z], h_ss.at[j], h_rs.at[z], 4 * j + sub, v)

    def h_from(j):
        return remote(hs.at[j], hr.at[j], h_ss.at[j], h_rs.at[j], 4 * j + sub, v)

    def b_copy(j):
        return remote(br.at[z], br.at[z], b_ss.at[j], b_rs.at[z], 4 * j + sub, v)

    def b_from(j):
        return remote(br.at[z], br.at[j], b_ss.at[j], b_rs.at[j], 4 * j + sub, v)

    def c1(j):
        return remote(crs.at[pl.ds(4 * j, 4)], crr.at[pl.ds(4 * z, 4)], c_ss.at[j], c_rs.at[z], 4 * j + sub, v)

    def c1_from(j):
        four = pl.ds(4 * j, 4)
        return remote(crs.at[four], crr.at[four], c_ss.at[j], c_rs.at[j], 4 * j + sub, v)

    def c2(k):
        return remote(cmid.at[k], crt.at[sub], c_ss.at[4 + k], c_rs.at[4 + sub], 4 * z + k, v)

    def c2_from(k):
        return remote(cmid.at[k], crt.at[k], c_ss.at[4 + k], c_rs.at[4 + k], 4 * z + k, v)

    def f1(k):
        return remote(cfall.at[s], cfall.at[s], f_ss.at[k], f_rs.at[sub], 4 * z + k, v)

    def f1_from(k):
        return remote(cfall.at[s], cfall.at[4 * z + k], f_ss.at[k], f_rs.at[k], 4 * z + k, v)

    def f2(j):
        four = cfall.at[pl.ds(4 * z, 4)]
        return remote(four, four, f_ss.at[4 + j], f_rs.at[4 + z], 4 * j + sub, v)

    def f2_from(j):
        four = cfall.at[pl.ds(4 * j, 4)]
        return remote(four, four, f_ss.at[4 + j], f_rs.at[4 + j], 4 * j + sub, v)

    def beside(d):
        return lax.rem(sub + d, 4)

    def v_copy(j):
        to = 4 * z + lax.rem(j, 4)
        mine = ball.at[place]
        return remote(mine, mine, v_ss.at[j], v_rs.at[place], to, j // 4)

    def v_from(j):
        to = 4 * z + lax.rem(j, 4)
        return remote(ball.at[place], ball.at[j], v_ss.at[j], v_rs.at[j], to, j // 4)

    x_across(0).start()
    x_beside(0).start()
    each(4, lambda i: block_at(i), lambda j: p_copy(j).start())

    def products():
        beta = bet[:, 0:64]
        b_hi = beta.astype(BF16).astype(F32)
        rest = beta - b_hi
        b_mid = rest.astype(BF16).astype(F32)
        none = jnp.zeros_like(beta)
        rows = jnp.concatenate([b_hi, b_mid, rest - b_mid, none], axis=0)
        rows = jnp.concatenate([rows, rows], axis=1).astype(BF16)
        eta = dot(rows, xhl[...])
        eta = eta[0:8] + eta[8:16] + eta[16:24]
        fitted = 1.0 / (1.0 + jnp.exp(-eta))
        coded = y4[...]
        seen = coded >= 0.0
        wbuf[...] = jnp.where(seen, fitted * (1.0 - fitted), 0.0)
        work = jnp.where(seen, coded - fitted, 0.0)
        r_hi = work.astype(BF16).astype(F32)
        rest = work - r_hi
        r_mid = rest.astype(BF16).astype(F32)
        none = jnp.zeros_like(work)
        lhs[512:544, :] = jnp.concatenate([r_hi, r_mid, rest - r_mid, none], axis=0).astype(BF16)

        @pl.loop(0, 16)
        def _(i):
            cols = pl.ds(pl.multiple_of(i * 512, 512), 512)
            table = xt4[:, cols]
            for p in range(8):
                lhs[p * 64 : (p + 1) * 64, cols] = (table * wbuf[p : p + 1, cols]).astype(BF16)

        hacc[...] = fold(exact_t(lhs[...], xhl[...]))

    def products0(side):
        wide = pl.ds(pl.multiple_of(side * 4096, 4096), 4096)
        coded = y4[:, wide]
        seen = coded >= 0.0
        wbuf[:, wide] = jnp.where(seen, 0.25, 0.0)
        work = jnp.where(seen, coded - 0.5, 0.0)
        r_hi = work.astype(BF16).astype(F32)
        rest = work - r_hi
        r_mid = rest.astype(BF16).astype(F32)
        none = jnp.zeros_like(work)
        lhs[512:544, wide] = jnp.concatenate([r_hi, r_mid, rest - r_mid, none], axis=0).astype(BF16)

        @pl.loop(0, 8)
        def _(i):
            cols = pl.ds(pl.multiple_of(side * 4096 + i * 512, 512), 512)
            table = xhl[0:64, cols].astype(F32)
            for p in range(8):
                lhs[p * 64 : (p + 1) * 64, cols] = (table * wbuf[p : p + 1, cols]).astype(BF16)

        out = exact_t(lhs[:, wide], xhl[0:64, wide])
        return jnp.concatenate([out, out], axis=1)

    def send_sums():
        grads = hacc[512:520, :] + hacc[520:528, :] + hacc[528:536, :]
        line = lax.broadcasted_iota(jnp.int32, (4, 1), 0)

        def one(j):
            first = hacc[pl.ds(pl.multiple_of(j * 64, 64), 64), :]
            second = hacc[pl.ds(pl.multiple_of((j + nz) * 64, 64), 64), :]
            hs[j, 0:64, :] = jnp.where(low, first, second)
            pair = jnp.where(low, grads[0:4], grads[4:8])
            hs[j, 64:65, :] = jnp.sum(jnp.where(line == j, pair, 0.0), axis=0, keepdims=True)

        for d in (2, 1, 3):
            one(zpeer(d))
            h_copy(zpeer(d)).start()
        one(z)

    def crosses():
        @pl.loop(0, 8)
        def _(t):
            out = dot(xhl[:, own], gbuf[:, pl.ds(pl.multiple_of(t * 256, 256), 256)])
            out = out[0:64] + out[64:128]
            crs[2 * t] = out[:, 0:128]
            crs[2 * t + 1] = out[:, 128:256]

    def upright():
        @pl.loop(0, 16)
        def _(i):
            at = pl.ds(pl.multiple_of(i * 128, 128), 128)
            from_ = pl.ds(pl.multiple_of(sub * 2048 + i * 128, 128), 128)
            both = xhl[:, from_].astype(F32).T.astype(BF16)
            x4[at, 0:128] = both
            x4[at, 128:256] = both

    def project(t):
        for h in range(2):
            part = cfall[2 * t + h]
            cols = slice(h * 128, (h + 1) * 128)
            c4[0:64, cols] = part[0:64]
            c4[64:128, cols] = part[0:64]
            c4[128:192, cols] = part[64:128]
            c4[192:256, cols] = part[64:128]
        cols = pl.ds(pl.multiple_of(t * PROJ, PROJ), PROJ)

        @pl.loop(0, 2048 // ROWS)
        def _(i):
            rows = pl.ds(pl.multiple_of(i * ROWS, ROWS), ROWS)
            proj = gbuf[rows, cols].astype(F32) - dot(x4[rows, :], c4[...])
            gbuf[rows, cols] = proj.astype(BF16)
            psq[rows, cols] = (proj * proj).astype(BF16)

    def total_sums():
        total = hs[z]
        for d in (1, 3, 2):
            h_from(zpeer(d)).wait_recv()
            total = total + hr[zpeer(d)]
        return total

    def share(delta):
        bcur[0:1, :] = bcur[0:1, :] + delta
        br[z] = bcur[...]
        for d in (2, 1, 3):
            b_copy(zpeer(d)).start()

    def collect():
        for d in (1, 3, 2):
            b_from(zpeer(d)).wait_recv()
        rows = br[:, 0, :]
        bet[...] = jnp.concatenate([rows, pltpu.roll(rows, 64, 1)], axis=0)
        for d in (1, 2, 3):
            h_copy(zpeer(d)).wait_send()

    gcopy.wait()
    crosses()
    x_from(0, 1).wait_recv()
    p_from(block_at(1)).wait_recv()
    hacc[...] = products0(xh)
    x_from(0, 2).wait_recv()
    x_relay(0).start()
    for d in (1, 2, 3):
        pl.semaphore_signal(
            told, inc=1, device_id=(4 * z + lax.rem(sub + d, 4), v), device_id_type=mesh_id
        )
    x_across(1).start()
    x_beside(1).start()
    upright()
    p_from(block_at(2)).wait_recv()
    p_from(block_at(3)).wait_recv()
    x_from(0, 3).wait_recv()
    hacc[...] += products0(1 - xh)
    send_sums()
    x_from(1, 2).wait_recv()
    x_relay(1).start()
    join(block_at(2))
    x_from(1, 1).wait_recv()
    join(block_at(1))
    x_from(1, 3).wait_recv()
    join(block_at(3))
    pl.semaphore_wait(told, 3)
    share(sweep(total_sums(), False))
    gram = exact_t(xhl[...], xhl[...])
    grs[...] = fold(gram[0:64, :] + gram[64:128, :])
    for d in (2, 1, 3):
        gr_copy(zpeer(d)).start()
    collect()
    for d in (2, 1, 3):
        c1(zpeer(d)).start()

    @pl.loop(1, ITERS)
    def _(it):
        products()
        send_sums()

        @pl.when(it == 1)
        def _():
            gram = grs[...]
            for d in (1, 3, 2):
                gr_from(zpeer(d)).wait_recv()
                gram = gram + grr[zpeer(d)]
            ginv_ref[...] = sweep(gram, True)
            for d in (1, 3, 2):
                c1_from(zpeer(d)).wait_recv()
            for k in range(4):
                piece = crs[4 * z + k]
                for d in (1, 3, 2):
                    piece = piece + crr[4 * zpeer(d) + k]
                cmid[k] = piece
            for d in (1, 2, 3):
                c2(beside(d)).start()

        @pl.when(it == 3)
        def _():
            for d in (1, 3, 2):
                f2_from(zpeer(d)).wait_recv()

            @pl.loop(0, 3)
            def _(t):
                project(t)

        delta = sweep(total_sums(), False)
        each(nz, zpeer, lambda j: b_copy(j).wait_send())
        share(delta)

        @pl.when(it == 1)
        def _():
            cross = cmid[sub]
            for d in (1, 2, 3):
                c2_from(beside(d)).wait_recv()
                cross = cross + crt[beside(d)]
            hi, lo = two(exact(-ginv_ref[:, 0:64], cross))
            cfall[s, 0:64, :] = hi
            cfall[s, 64:128, :] = lo
            for d in (1, 2, 3):
                f1(beside(d)).start()
            each(nv, vpeer, lambda j: y_copy(j).start())

        @pl.when(it == 2)
        def _():
            for d in (1, 2, 3):
                f1_from(beside(d)).wait_recv()
            for d in (2, 1, 3):
                f2(zpeer(d)).start()

        @pl.when(it == 3)
        def _():
            @pl.loop(3, 6)
            def _(t):
                project(t)

        collect()

    ball[place] = bet[...]
    each(plane, ppeer, lambda j: v_copy(j).start())
    yall[v] = ybuf[...]

    @pl.loop(6, 8)
    def _(t):
        project(t)

    @pl.loop(0, nv)
    def _(d):
        u = lax.rem(v + nv - d, nv)

        @pl.when(d == 0)
        def _():
            for k in (1, 2, 3):
                v_from(4 * v + lax.rem(sub + k, 4)).wait_recv()

        @pl.when(d > 0)
        def _():
            y_from(u).wait_recv()
            for k in range(4):
                v_from(4 * u + k).wait_recv()

        rows = ball[pl.ds(u * 4, 4)].reshape(32, 128)
        eta = exact(rows[:, 0:64], xt_ref[...])
        fitted = 1.0 / (1.0 + jnp.exp(-eta))
        coded = yall[u]
        seen = coded >= 0.0
        resid = jnp.where(seen, coded - fitted, 0.0).astype(BF16)
        wslab = jnp.where(seen, fitted * (1.0 - fitted), 0.0).astype(BF16)
        wide = resid.astype(F32)
        square = (wide * wide).astype(BF16)
        for h in range(2):
            half = slice(h * 16, (h + 1) * 16)
            at = pl.multiple_of(u * 16 + h * 128, 16)
            r1[pl.ds(at, 16), :] = resid[half]
            r2[pl.ds(at, 16), :] = square[half]
            r2[pl.ds(at + 256, 16), :] = wslab[half]

    width = 2048 // TILES

    def a_copy(t):
        return remote(asd.at[t], arv.at[t], a_ss.at[t], a_rs.at[t], s + 1 - 2 * core, v)

    def z1(t, j):
        pair = bsd.at[t, pl.ds(2 * j, 2)]
        return remote(pair, brv.at[t, pl.ds(2 * z, 2)], q_ss.at[t, j], q_rs.at[t, z], 4 * j + sub, v)

    def z1_from(t, j):
        pair = bsd.at[t, pl.ds(2 * j, 2)]
        return remote(pair, brv.at[t, pl.ds(2 * j, 2)], q_ss.at[t, j], q_rs.at[t, j], 4 * j + sub, v)

    def x1(t):
        four = pl.ds(4 * (1 - xh), 4)
        return remote(bsd.at[t, four], brv.at[t, four], q_ss.at[t, 4], q_rs.at[t, 4], across, v)

    def x1_from(t):
        four = pl.ds(4 * xh, 4)
        return remote(bsd.at[t, four], brv.at[t, four], q_ss.at[t, 4], q_rs.at[t, 4], across, v)

    def x2(t):
        return remote(lsd.at[t, 0], lrv.at[t, 0], w_ss.at[t, 4], w_rs.at[t, 4], across, v)

    def z2(t, j):
        return remote(lsd.at[t, j], lrv.at[t, z], w_ss.at[t, j], w_rs.at[t, z], 4 * j + sub, v)

    def z2_from(t, j):
        return remote(lsd.at[t, j], lrv.at[t, j], w_ss.at[t, j], w_rs.at[t, j], 4 * j + sub, v)

    def stage1(b):
        slot = lax.rem(b, 2)
        a_copy(b).wait_recv()

        def total(zz, xx):
            at = pl.multiple_of(core * 128 + (2 * zz + xx) * 16, 16)
            other = arv[b, 2 * zz + xx].astype(F32)
            score = so[slot, pl.ds(at, 16), :] + other[0:16] + other[16:32]
            robust = so[slot, pl.ds(at + 256, 16), :] + other[32:48]
            model = so[slot, pl.ds(at + 512, 16), :] + other[48:64]
            return jnp.concatenate([score, robust, model], axis=0)

        @pl.when(lax.rem(b, 2) == 0)
        def _():
            for d in (2, 1, 3):
                j = zpeer(d)
                for xx in range(2):
                    bsd[b, 2 * j + xx] = total(j, xx).astype(BF16)
                z1(b, j).start()
            for xx in range(2):
                keep[b, xx] = total(z, xx)

        @pl.when(lax.rem(b, 2) == 1)
        def _():
            for j in range(nz):
                bsd[b, 4 * (1 - xh) + j] = total(j, 1 - xh).astype(BF16)
            x1(b).start()
            for j in range(nz):
                keep[b, j] = total(j, xh)

    def stage2(b):
        @pl.when(lax.rem(b, 2) == 0)
        def _():
            for d in (1, 3, 2):
                z1_from(b, zpeer(d)).wait_recv()

            def total(xx):
                out = keep[b, xx]
                for d in (1, 2, 3):
                    out = out + brv[b, 2 * zpeer(d) + xx].astype(F32)
                return out

            lsd[b, 0] = total(1 - xh).astype(BF16)
            x2(b).start()
            fin[b] = total(xh)

        @pl.when(lax.rem(b, 2) == 1)
        def _():
            x1_from(b).wait_recv()

            def total(j):
                return keep[b, j] + brv[b, 4 * xh + j].astype(F32)

            for d in (2, 1, 3):
                j = zpeer(d)
                lsd[b, j] = total(j).astype(BF16)
                z2(b, j).start()
            fin[b] = total(z)

    @pl.loop(0, TILES + LAG)
    def _(t):
        @pl.when(t < TILES)
        def _():
            slot = lax.rem(t, 2)
            cols = pl.ds(pl.multiple_of(t * width, width), width)
            so[slot, 0:256, :] = dot(r1[...], gbuf[:, cols])
            so[slot, 256:768, :] = dot(r2[...], psq[:, cols])

            @pl.loop(0, ns // 2)
            def _(q):
                at = pl.multiple_of((1 - core) * 128 + q * 16, 16)
                hi, lo = two(so[slot, pl.ds(at, 16), :])
                asd[t, q, 0:16, :] = hi
                asd[t, q, 16:32, :] = lo
                asd[t, q, 32:48, :] = so[slot, pl.ds(at + 256, 16), :].astype(BF16)
                asd[t, q, 48:64, :] = so[slot, pl.ds(at + 512, 16), :].astype(BF16)

            a_copy(t).start()

        @pl.when((t > 0) & (t <= TILES))
        def _():
            stage1(t - 1)

        @pl.when(t >= LAG)
        def _():
            stage2(t - LAG)

    for low_part in range(2):
        x_across(low_part).wait_send()
        x_beside(low_part).wait_send()
        x_relay(low_part).wait_send()
    each(4, lambda i: block_at(i), lambda j: p_copy(j).wait_send())
    each(nz, zpeer, lambda j: b_copy(j).wait_send())
    each(nz, zpeer, lambda j: gr_copy(j).wait_send())
    for d in (1, 2, 3):
        c1(zpeer(d)).wait_send()
        c2(beside(d)).wait_send()
        f1(beside(d)).wait_send()
        f2(zpeer(d)).wait_send()
    each(nv, vpeer, lambda j: y_copy(j).wait_send())
    each(plane, ppeer, lambda j: v_copy(j).wait_send())

    for t in range(TILES):
        total = fin[t]
        if t % 2 == 0:
            x2(t).wait_recv()
            total = total + lrv[t, 0].astype(F32)
        else:
            for d in (1, 3, 2):
                z2_from(t, zpeer(d)).wait_recv()
                total = total + lrv[t, zpeer(d)].astype(F32)
        tot_ref[:, t * width : (t + 1) * width] = total

    for t in range(TILES):
        a_copy(t).wait_send()
        if t % 2 == 0:
            x2(t).wait_send()
            for d in (1, 2, 3):
                z1(t, zpeer(d)).wait_send()
        else:
            x1(t).wait_send()
            for d in (1, 2, 3):
                z2(t, zpeer(d)).wait_send()


def per_device(ns, nv, genotype, covariates, outcome, cohort, measured):
    vm = pltpu.VMEM
    dma = pltpu.SemaphoreType.DMA
    width = 2048 // TILES
    nz = ns // 4
    scratch = [
        vm((2048, 2048), BF16),
        vm((2048, 2048), BF16),
        vm((64, 8192), F32),
        vm((128, 8192), BF16),
        vm((2048, 256), BF16),
        vm((32, 2048), F32),
        vm((8, 8192), F32),
        vm((nv, 32, 2048), F32),
        vm((8, 8192), F32),
        vm((544, 8192), BF16),
        vm((544, 128), F32),
        vm((nz, 72, 128), F32),
        vm((nz, 72, 128), F32),
        vm((ns, 64, 128), F32),
        vm((ns, 64, 128), F32),
        vm((4, 64, 128), F32),
        vm((4, 64, 128), F32),
        vm((64, 128), F32),
        vm((nz, 64, 128), F32),
        vm((64, 128), F32),
        vm((8, 128), F32),
        vm((nz, 8, 128), F32),
        vm((8, 128), F32),
        vm((4 * nv, 8, 128), F32),
        vm((256, PROJ), BF16),
        vm((ns, 128, 128), BF16),
        vm((256, 2048), BF16),
        vm((512, 2048), BF16),
        vm((2, 768, width), F32),
        vm((TILES, ns // 2, 64, width), BF16),
        vm((TILES, ns // 2, 64, width), BF16),
        vm((TILES, ns // 2, 48, width), BF16),
        vm((TILES, ns // 2, 48, width), BF16),
        vm((TILES, 4, 48, width), F32),
        vm((TILES, 4, 48, width), BF16),
        vm((TILES, 4, 48, width), BF16),
        vm((TILES, 48, width), F32),
        dma,
    ]
    scratch += [dma((ns,))] * 4 + [dma((nz,))] * 6 + [dma((4,))] * 6 + [dma((nv,))] * 2
    scratch += [dma((4 * nv,))] * 2 + [dma((TILES,))] * 2 + [dma((TILES, ns // 2))] * 4
    scratch.append(pltpu.SemaphoreType.REGULAR)
    inside = pl.BlockSpec(memory_space=pltpu.VMEM)
    totals = pl.pallas_call(
        functools.partial(kernel, ns, nv),
        out_shape=jax.ShapeDtypeStruct((48, 2048), F32),
        in_specs=[pl.BlockSpec(memory_space=pl.ANY)] + [inside] * 4,
        out_specs=inside,
        scratch_shapes=scratch,
        compiler_params=pltpu.CompilerParams(
            collective_id=0, has_side_effects=True, vmem_limit_bytes=60 * 2**20
        ),
        name="score_tests",
    )(genotype, covariates.T, outcome.T, cohort[None, :], measured.T)
    score, robust, model = totals[0:16], totals[16:32], totals[32:48]
    return score * lax.rsqrt(robust + EPS), score * lax.rsqrt(model + EPS)


def solution(mesh):
    placed = (
        P("sample", "variant"),
        P("sample", None),
        P("sample", "variant"),
        P("sample"),
        P("variant", None),
    )
    return jax.shard_map(
        functools.partial(per_device, mesh.shape["sample"], mesh.shape["variant"]),
        mesh=mesh,
        in_specs=placed,
        out_specs=(P("sample", "variant"), P("sample", "variant")),
        check_vma=False,
    )
```

```python
import functools

import jax
import jax.numpy as jnp
from jax import lax
from jax.experimental import pallas as pl
from jax.experimental.pallas import tpu as pltpu
from jax.sharding import PartitionSpec as P

ITERS = 4
EPS = 1e-06
HIGHEST = lax.Precision.HIGHEST
F32 = jnp.float32
BF16 = jnp.bfloat16
LAG = 6
TILES = 8
PROJ = 256
ROWS = 512


def dot(a, b):
    return jnp.dot(a, b, preferred_element_type=F32)


def exact(a, b):
    return jnp.dot(a, b, preferred_element_type=F32, precision=HIGHEST)


def two(x):
    hi = x.astype(BF16)
    return hi, (x - hi.astype(F32)).astype(BF16)


def fold(x):
    return x + pltpu.roll(x, 64, 1)


def exact_t(a, b):
    return lax.dot_general(a, b, (((1,), (1,)), ((), ())), preferred_element_type=F32)


def linear(beta, table):
    n = beta.shape[0]
    hi = beta.astype(BF16).astype(F32)
    rest = beta - hi
    mid = rest.astype(BF16).astype(F32)
    rows = jnp.concatenate([hi, mid, rest - mid, jnp.zeros_like(beta)], axis=0)
    rows = jnp.concatenate([rows, rows], axis=1).astype(BF16)
    out = dot(rows, table)
    return out[0:n] + out[n : 2 * n] + out[2 * n : 3 * n]


def product(x, y):
    out = []
    for i in range(len(x)):
        line = []
        for j in range(len(y[0])):
            term = x[i][0] * y[0][j]
            for k in range(1, len(y)):
                term = term + x[i][k] * y[k][j]
            line.append(term)
        out.append(line)
    return out


def inverse2(a):
    (p, q), (_, d) = a
    i = 1.0 / (p * d - q * q)
    return [[d * i, -(q * i)], [-(q * i), p * i]]


def inverse4(a):
    right = [r[2:] for r in a[:2]]
    corner = [r[2:] for r in a[2:]]
    flip = lambda x: [list(c) for c in zip(*x)]
    first = inverse2([r[:2] for r in a[:2]])
    lead = product(first, right)
    inner = product(flip(right), lead)
    last = inverse2([[corner[i][j] - inner[i][j] for j in range(2)] for i in range(2)])
    side = product(lead, last)
    more = product(side, flip(lead))
    top = [[first[i][j] + more[i][j] for j in range(2)] + [-side[i][j] for j in range(2)] for i in range(2)]
    return top + [[-side[j][i] for j in range(2)] + last[i] for i in range(2)]


def sweep(m, full):
    lane = lax.broadcasted_iota(jnp.int32, (1, 128), 1)
    low = lane < 64
    place = jnp.where(low, lane, lane - 64)
    height = lax.broadcasted_iota(jnp.int32, (64, 1), 0)
    for k in range(0, 64, 4):
        if not full and k % 8 == 0 and k:
            m = m[8:, :]
        r = k if full else k % 8
        cols = [jnp.where(low, m[:, k + j : k + j + 1], m[:, 64 + k + j : 65 + k + j]) for j in range(4)]
        pivot = [[cols[max(i, j)][r + min(i, j) : r + min(i, j) + 1, :] for j in range(4)] for i in range(4)]
        here = (place >= k) & (place < k + 4)
        lines = [
            [jnp.where(here, jnp.where(place == k + j, -1.0, 0.0), m[r + j : r + j + 1, :])] for j in range(4)
        ]
        lines = product(inverse4(pivot), lines)
        m = jnp.where(here, 0.0, m)
        if full:
            mine = (height >= k) & (height < k + 4)
            m = jnp.where(mine, 0.0, m)
            cols = [jnp.where(mine, jnp.where(height == k + j, -1.0, 0.0), cols[j]) for j in range(4)]
        m = m - product([cols], lines)[0][0]
    return m if full else m[8:9, :]


def kernel(
    ns,
    nv,
    g_hbm,
    xt_ref,
    out_ref,
    cohort_ref,
    meas_ref,
    tot_ref,
    gbuf,
    psq,
    xt4,
    xhl,
    x4,
    ybuf,
    y4,
    yall,
    wbuf,
    lhs,
    hacc,
    hs,
    hr,
    crs,
    crr,
    cmid,
    crt,
    grs,
    grr,
    ginv_ref,
    bcur,
    br,
    bet,
    ball,
    c4,
    cfall,
    r1,
    r2,
    so,
    asd,
    arv,
    bsd,
    brv,
    keep,
    lsd,
    lrv,
    fin,
    g_sem,
    c_ss,
    c_rs,
    f_ss,
    f_rs,
    h_ss,
    h_rs,
    gr_ss,
    gr_rs,
    b_ss,
    b_rs,
    x_ss,
    x_rs,
    l_ss,
    l_rs,
    p_ss,
    p_rs,
    y_ss,
    y_rs,
    v_ss,
    v_rs,
    a_ss,
    a_rs,
    q_ss,
    q_rs,
    w_ss,
    w_rs,
    told,
):
    nz = ns // 4
    s = lax.axis_index("sample")
    v = lax.axis_index("variant")
    z = s // 4
    sub = lax.rem(s, 4)
    core = lax.rem(s, 2)
    xh = sub // 2
    sibling = s + 1 - 2 * core
    across = s + 2 - 4 * xh
    near = v + 1 - 2 * lax.rem(v, 2)
    low = lax.broadcasted_iota(jnp.int32, (1, 128), 1) < 64
    mesh_id = pl.DeviceIdType.MESH

    gcopy = pltpu.make_async_copy(g_hbm, gbuf, g_sem)
    gcopy.start()

    def block(b):
        return pl.ds(pl.multiple_of(b * 2048, 2048), 2048)

    def split(b):
        hi, lo = two(xt4[:, block(b)])
        xhl[0:64, block(b)] = hi
        xhl[64:128, block(b)] = lo

    def join(b):
        xt4[:, block(b)] = xhl[0:64, block(b)].astype(F32) + xhl[64:128, block(b)].astype(F32)

    def block_at(i):
        return 2 * lax.rem(xh + i // 2, 2) + lax.rem(core + i, 2)

    def zpeer(d):
        return lax.rem(z + d, nz)

    def vpeer(d):
        return lax.rem(v + d, nv)

    def remote(src, dst, ss, rs, sample, variant):
        return pltpu.make_async_remote_copy(
            src_ref=src,
            dst_ref=dst,
            send_sem=ss,
            recv_sem=rs,
            device_id=(sample, variant),
            device_id_type=mesh_id,
        )

    def each(n, peer, do):
        @pl.loop(1, n)
        def _(d):
            do(peer(d))

    barrier = pltpu.get_barrier_semaphore()

    def greet(sample, variant):
        pl.semaphore_signal(barrier, inc=1, device_id=(sample, variant), device_id_type=mesh_id)

    plane = 4 * nv
    place = v * 4 + sub

    def ppeer(d):
        return lax.rem(place + d, plane)

    greet(across, near)
    for d in (1, 2, 3):
        greet(4 * z + lax.rem(sub + d, 4), v)
    for d in (2, 1, 3):
        greet(4 * zpeer(d) + sub, v)
    for d in range(2, nv, 2):
        greet(s, vpeer(d))

    hot = lax.broadcasted_iota(jnp.int32, (16, 2048), 0) == cohort_ref[...]
    mask = lax.dot_general(
        meas_ref[...].astype(BF16),
        hot.astype(BF16),
        (((0,), (0,)), ((), ())),
        preferred_element_type=F32,
    )
    ybuf[...] = jnp.where(mask > 0.5, out_ref[...], -1.0)
    own = block(sub)
    y4[:, own] = ybuf[pl.ds(pl.multiple_of(sub * 8, 8), 8), :]
    xt4[:, own] = xt_ref[...]
    split(sub)
    bcur[...] = jnp.zeros_like(bcur)
    br[...] = jnp.zeros_like(br)
    bet[...] = jnp.zeros_like(bet)
    hs[...] = jnp.zeros_like(hs)

    pl.semaphore_wait(barrier, 7 + nv // 2 - 1)

    def part(low_part, b):
        return xhl.at[pl.ds(64 * low_part, 64), block(b)]

    def x_sems(low_part, i):
        return (l_ss.at[i], l_rs.at[i]) if low_part else (x_ss.at[i], x_rs.at[i])

    def x_beside(low_part):
        mine = part(low_part, sub)
        return remote(mine, mine, *x_sems(low_part, 1), sibling, v)

    def x_across(low_part):
        mine = part(low_part, sub)
        return remote(mine, mine, *x_sems(low_part, 2), across, near)

    def x_relay(low_part):
        theirs = part(low_part, block_at(2))
        return remote(theirs, theirs, *x_sems(low_part, 3), sibling, v)

    def x_from(low_part, i):
        theirs = part(low_part, block_at(i))
        return remote(theirs, theirs, *x_sems(low_part, i), sibling, v)

    def p_copy(j):
        rows = pl.ds(pl.multiple_of(j * 8, 8), 8)
        return remote(ybuf.at[rows], y4.at[:, own], p_ss.at[j], p_rs.at[sub], 4 * z + j, v)

    def p_from(j):
        rows = pl.ds(pl.multiple_of(j * 8, 8), 8)
        return remote(ybuf.at[rows], y4.at[:, block(j)], p_ss.at[j], p_rs.at[j], 4 * z + j, v)

    def y_copy(j):
        return remote(ybuf, yall.at[v], y_ss.at[j], y_rs.at[v], s, j)

    def y_from(j):
        return remote(ybuf, yall.at[j], y_ss.at[j], y_rs.at[j], s, j)

    def gr_copy(j):
        return remote(grs, grr.at[z], gr_ss.at[j], gr_rs.at[z], 4 * j + sub, v)

    def gr_from(j):
        return remote(grs, grr.at[j], gr_ss.at[j], gr_rs.at[j], 4 * j + sub, v)

    def h_copy(j):
        return remote(hs.at[j], hr.at[z], h_ss.at[j], h_rs.at[z], 4 * j + sub, v)

    def h_from(j):
        return remote(hs.at[j], hr.at[j], h_ss.at[j], h_rs.at[j], 4 * j + sub, v)

    def b_copy(j):
        return remote(br.at[z], br.at[z], b_ss.at[j], b_rs.at[z], 4 * j + sub, v)

    def b_from(j):
        return remote(br.at[z], br.at[j], b_ss.at[j], b_rs.at[j], 4 * j + sub, v)

    def c1(j):
        return remote(crs.at[pl.ds(4 * j, 4)], crr.at[pl.ds(4 * z, 4)], c_ss.at[j], c_rs.at[z], 4 * j + sub, v)

    def c1_from(j):
        four = pl.ds(4 * j, 4)
        return remote(crs.at[four], crr.at[four], c_ss.at[j], c_rs.at[j], 4 * j + sub, v)

    def c2(k):
        return remote(cmid.at[k], crt.at[sub], c_ss.at[4 + k], c_rs.at[4 + sub], 4 * z + k, v)

    def c2_from(k):
        return remote(cmid.at[k], crt.at[k], c_ss.at[4 + k], c_rs.at[4 + k], 4 * z + k, v)

    def f1(k):
        return remote(cfall.at[s], cfall.at[s], f_ss.at[k], f_rs.at[sub], 4 * z + k, v)

    def f1_from(k):
        return remote(cfall.at[s], cfall.at[4 * z + k], f_ss.at[k], f_rs.at[k], 4 * z + k, v)

    def f2(j):
        four = cfall.at[pl.ds(4 * z, 4)]
        return remote(four, four, f_ss.at[4 + j], f_rs.at[4 + z], 4 * j + sub, v)

    def f2_from(j):
        four = cfall.at[pl.ds(4 * j, 4)]
        return remote(four, four, f_ss.at[4 + j], f_rs.at[4 + j], 4 * j + sub, v)

    def beside(d):
        return lax.rem(sub + d, 4)

    def v_copy(j):
        to = 4 * z + lax.rem(j, 4)
        mine = ball.at[place]
        return remote(mine, mine, v_ss.at[j], v_rs.at[place], to, j // 4)

    def v_from(j):
        to = 4 * z + lax.rem(j, 4)
        return remote(ball.at[place], ball.at[j], v_ss.at[j], v_rs.at[j], to, j // 4)

    x_across(0).start()
    x_beside(0).start()
    each(4, lambda i: block_at(i), lambda j: p_copy(j).start())

    def products():
        eta = linear(bet[:, 0:64], xhl[...])
        fitted = 1.0 / (1.0 + jnp.exp(-eta))
        coded = y4[...]
        seen = coded >= 0.0
        wbuf[...] = jnp.where(seen, fitted * (1.0 - fitted), 0.0)
        work = jnp.where(seen, coded - fitted, 0.0)
        r_hi = work.astype(BF16).astype(F32)
        rest = work - r_hi
        r_mid = rest.astype(BF16).astype(F32)
        none = jnp.zeros_like(work)
        lhs[512:544, :] = jnp.concatenate([r_hi, r_mid, rest - r_mid, none], axis=0).astype(BF16)

        @pl.loop(0, 16)
        def _(i):
            cols = pl.ds(pl.multiple_of(i * 512, 512), 512)
            table = xt4[:, cols]
            for p in range(8):
                lhs[p * 64 : (p + 1) * 64, cols] = (table * wbuf[p : p + 1, cols]).astype(BF16)

        hacc[...] = fold(exact_t(lhs[...], xhl[...]))

    def products0(side):
        wide = pl.ds(pl.multiple_of(side * 4096, 4096), 4096)
        coded = y4[:, wide]
        seen = coded >= 0.0
        wbuf[:, wide] = jnp.where(seen, 0.25, 0.0)
        work = jnp.where(seen, coded - 0.5, 0.0)
        r_hi = work.astype(BF16).astype(F32)
        rest = work - r_hi
        r_mid = rest.astype(BF16).astype(F32)
        none = jnp.zeros_like(work)
        lhs[512:544, wide] = jnp.concatenate([r_hi, r_mid, rest - r_mid, none], axis=0).astype(BF16)

        @pl.loop(0, 8)
        def _(i):
            cols = pl.ds(pl.multiple_of(side * 4096 + i * 512, 512), 512)
            table = xhl[0:64, cols].astype(F32)
            for p in range(8):
                lhs[p * 64 : (p + 1) * 64, cols] = (table * wbuf[p : p + 1, cols]).astype(BF16)

        out = exact_t(lhs[:, wide], xhl[0:64, wide])
        return jnp.concatenate([out, out], axis=1)

    def send_sums():
        grads = hacc[512:520, :] + hacc[520:528, :] + hacc[528:536, :]
        line = lax.broadcasted_iota(jnp.int32, (4, 1), 0)

        def one(j):
            first = hacc[pl.ds(pl.multiple_of(j * 64, 64), 64), :]
            second = hacc[pl.ds(pl.multiple_of((j + nz) * 64, 64), 64), :]
            hs[j, 0:64, :] = jnp.where(low, first, second)
            pair = jnp.where(low, grads[0:4], grads[4:8])
            hs[j, 64:65, :] = jnp.sum(jnp.where(line == j, pair, 0.0), axis=0, keepdims=True)

        for d in (2, 1, 3):
            one(zpeer(d))
            h_copy(zpeer(d)).start()
        one(z)

    def crosses():
        @pl.loop(0, 8)
        def _(t):
            out = dot(xhl[:, own], gbuf[:, pl.ds(pl.multiple_of(t * 256, 256), 256)])
            out = out[0:64] + out[64:128]
            crs[2 * t] = out[:, 0:128]
            crs[2 * t + 1] = out[:, 128:256]

    def upright():
        @pl.loop(0, 16)
        def _(i):
            at = pl.ds(pl.multiple_of(i * 128, 128), 128)
            from_ = pl.ds(pl.multiple_of(sub * 2048 + i * 128, 128), 128)
            both = xhl[:, from_].astype(F32).T.astype(BF16)
            x4[at, 0:128] = both
            x4[at, 128:256] = both

    def project(t):
        for h in range(2):
            part = cfall[2 * t + h]
            cols = slice(h * 128, (h + 1) * 128)
            c4[0:64, cols] = part[0:64]
            c4[64:128, cols] = part[0:64]
            c4[128:192, cols] = part[64:128]
            c4[192:256, cols] = part[64:128]
        cols = pl.ds(pl.multiple_of(t * PROJ, PROJ), PROJ)

        @pl.loop(0, 2048 // ROWS)
        def _(i):
            rows = pl.ds(pl.multiple_of(i * ROWS, ROWS), ROWS)
            proj = gbuf[rows, cols].astype(F32) - dot(x4[rows, :], c4[...])
            gbuf[rows, cols] = proj.astype(BF16)
            psq[rows, cols] = (proj * proj).astype(BF16)

    def total_sums():
        total = hs[z]
        for d in (1, 3, 2):
            h_from(zpeer(d)).wait_recv()
            total = total + hr[zpeer(d)]
        return total

    def share(delta):
        bcur[0:1, :] = bcur[0:1, :] + delta
        br[z] = bcur[...]
        for d in (2, 1, 3):
            b_copy(zpeer(d)).start()

    def collect():
        for d in (1, 3, 2):
            b_from(zpeer(d)).wait_recv()
        rows = br[:, 0, :]
        bet[...] = jnp.concatenate([rows, pltpu.roll(rows, 64, 1)], axis=0)

    gcopy.wait()
    crosses()
    x_from(0, 1).wait_recv()
    p_from(block_at(1)).wait_recv()
    hacc[...] = products0(xh)
    x_from(0, 2).wait_recv()
    x_relay(0).start()
    for d in (1, 2, 3):
        pl.semaphore_signal(
            told, inc=1, device_id=(4 * z + lax.rem(sub + d, 4), v), device_id_type=mesh_id
        )
    x_across(1).start()
    upright()
    p_from(block_at(2)).wait_recv()
    p_from(block_at(3)).wait_recv()
    x_from(0, 3).wait_recv()
    x_beside(1).start()
    hacc[...] += products0(1 - xh)
    send_sums()
    x_from(1, 2).wait_recv()
    x_relay(1).start()
    join(block_at(2))
    x_from(1, 1).wait_recv()
    join(block_at(1))
    x_from(1, 3).wait_recv()
    join(block_at(3))
    pl.semaphore_wait(told, 3)
    share(sweep(total_sums(), False))
    gram = exact_t(xhl[...], xhl[...])
    grs[...] = fold(gram[0:64, :] + gram[64:128, :])
    for d in (2, 1, 3):
        gr_copy(zpeer(d)).start()
    collect()
    for d in (2, 1, 3):
        c1(zpeer(d)).start()

    @pl.loop(1, ITERS)
    def _(it):
        products()
        for d in (1, 2, 3):
            h_copy(zpeer(d)).wait_send()
        send_sums()

        @pl.when(it == 1)
        def _():
            gram = grs[...]
            for d in (1, 3, 2):
                gr_from(zpeer(d)).wait_recv()
                gram = gram + grr[zpeer(d)]
            ginv_ref[...] = sweep(gram, True)
            for d in (1, 3, 2):
                c1_from(zpeer(d)).wait_recv()
            for k in range(4):
                piece = crs[4 * z + k]
                for d in (1, 3, 2):
                    piece = piece + crr[4 * zpeer(d) + k]
                cmid[k] = piece
            for d in (1, 2, 3):
                c2(beside(d)).start()

        @pl.when(it == 3)
        def _():
            for d in (1, 3, 2):
                f2_from(zpeer(d)).wait_recv()

            @pl.loop(0, 3)
            def _(t):
                project(t)

        delta = sweep(total_sums(), False)
        each(nz, zpeer, lambda j: b_copy(j).wait_send())
        share(delta)

        @pl.when(it == 1)
        def _():
            cross = cmid[sub]
            for d in (1, 2, 3):
                c2_from(beside(d)).wait_recv()
                cross = cross + crt[beside(d)]
            hi, lo = two(exact(-ginv_ref[:, 0:64], cross))
            cfall[s, 0:64, :] = hi
            cfall[s, 64:128, :] = lo
            for d in (1, 2, 3):
                f1(beside(d)).start()
            each(nv, vpeer, lambda j: y_copy(j).start())

        @pl.when(it == 2)
        def _():
            for d in (1, 2, 3):
                f1_from(beside(d)).wait_recv()
            for d in (2, 1, 3):
                f2(zpeer(d)).start()

        @pl.when(it == 3)
        def _():
            @pl.loop(3, 6)
            def _(t):
                project(t)

        collect()

    for d in (1, 2, 3):
        h_copy(zpeer(d)).wait_send()
    ball[place] = bet[...]
    each(plane, ppeer, lambda j: v_copy(j).start())
    yall[v] = ybuf[...]

    @pl.loop(6, 8)
    def _(t):
        project(t)

    @pl.loop(0, nv)
    def _(d):
        u = lax.rem(v + nv - d, nv)

        @pl.when(d == 0)
        def _():
            for k in (1, 2, 3):
                v_from(4 * v + lax.rem(sub + k, 4)).wait_recv()

        @pl.when(d > 0)
        def _():
            y_from(u).wait_recv()
            for k in range(4):
                v_from(4 * u + k).wait_recv()

        rows = ball[pl.ds(u * 4, 4)].reshape(32, 128)
        eta = linear(rows[:, 0:64], xhl[:, own])
        fitted = 1.0 / (1.0 + jnp.exp(-eta))
        coded = yall[u]
        seen = coded >= 0.0
        resid = jnp.where(seen, coded - fitted, 0.0).astype(BF16)
        wslab = jnp.where(seen, fitted * (1.0 - fitted), 0.0).astype(BF16)
        wide = resid.astype(F32)
        square = (wide * wide).astype(BF16)
        for h in range(2):
            half = slice(h * 16, (h + 1) * 16)
            at = pl.multiple_of(u * 16 + h * 128, 16)
            r1[pl.ds(at, 16), :] = resid[half]
            r2[pl.ds(at, 16), :] = square[half]
            r2[pl.ds(at + 256, 16), :] = wslab[half]

    width = 2048 // TILES

    def a_copy(t):
        return remote(asd.at[t], arv.at[t], a_ss.at[t], a_rs.at[t], s + 1 - 2 * core, v)

    def z1(t, j):
        pair = bsd.at[t, pl.ds(2 * j, 2)]
        return remote(pair, brv.at[t, pl.ds(2 * z, 2)], q_ss.at[t, j], q_rs.at[t, z], 4 * j + sub, v)

    def z1_from(t, j):
        pair = bsd.at[t, pl.ds(2 * j, 2)]
        return remote(pair, brv.at[t, pl.ds(2 * j, 2)], q_ss.at[t, j], q_rs.at[t, j], 4 * j + sub, v)

    def x1(t):
        four = pl.ds(4 * (1 - xh), 4)
        return remote(bsd.at[t, four], brv.at[t, four], q_ss.at[t, 4], q_rs.at[t, 4], across, v)

    def x1_from(t):
        four = pl.ds(4 * xh, 4)
        return remote(bsd.at[t, four], brv.at[t, four], q_ss.at[t, 4], q_rs.at[t, 4], across, v)

    def x2(t):
        return remote(lsd.at[t, 0], lrv.at[t, 0], w_ss.at[t, 4], w_rs.at[t, 4], across, v)

    def z2(t, j):
        return remote(lsd.at[t, j], lrv.at[t, z], w_ss.at[t, j], w_rs.at[t, z], 4 * j + sub, v)

    def z2_from(t, j):
        return remote(lsd.at[t, j], lrv.at[t, j], w_ss.at[t, j], w_rs.at[t, j], 4 * j + sub, v)

    def stage1(b):
        slot = lax.rem(b, 2)
        a_copy(b).wait_recv()

        def total(zz, xx):
            at = pl.multiple_of(core * 128 + (2 * zz + xx) * 16, 16)
            other = arv[b, 2 * zz + xx].astype(F32)
            score = so[slot, pl.ds(at, 16), :] + other[0:16] + other[16:32]
            robust = so[slot, pl.ds(at + 256, 16), :] + other[32:48]
            model = so[slot, pl.ds(at + 512, 16), :] + other[48:64]
            return jnp.concatenate([score, robust, model], axis=0)

        @pl.when(lax.rem(b, 2) == 0)
        def _():
            for d in (2, 1, 3):
                j = zpeer(d)
                for xx in range(2):
                    bsd[b, 2 * j + xx] = total(j, xx).astype(BF16)
                z1(b, j).start()
            for xx in range(2):
                keep[b, xx] = total(z, xx)

        @pl.when(lax.rem(b, 2) == 1)
        def _():
            for j in range(nz):
                bsd[b, 4 * (1 - xh) + j] = total(j, 1 - xh).astype(BF16)
            x1(b).start()
            for j in range(nz):
                keep[b, j] = total(j, xh)

    def stage2(b):
        @pl.when(lax.rem(b, 2) == 0)
        def _():
            for d in (1, 3, 2):
                z1_from(b, zpeer(d)).wait_recv()

            def total(xx):
                out = keep[b, xx]
                for d in (1, 2, 3):
                    out = out + brv[b, 2 * zpeer(d) + xx].astype(F32)
                return out

            lsd[b, 0] = total(1 - xh).astype(BF16)
            x2(b).start()
            fin[b] = total(xh)

        @pl.when(lax.rem(b, 2) == 1)
        def _():
            x1_from(b).wait_recv()

            def total(j):
                return keep[b, j] + brv[b, 4 * xh + j].astype(F32)

            for d in (2, 1, 3):
                j = zpeer(d)
                lsd[b, j] = total(j).astype(BF16)
                z2(b, j).start()
            fin[b] = total(z)

    @pl.loop(0, TILES + LAG)
    def _(t):
        @pl.when(t < TILES)
        def _():
            slot = lax.rem(t, 2)
            cols = pl.ds(pl.multiple_of(t * width, width), width)
            so[slot, 0:256, :] = dot(r1[...], gbuf[:, cols])
            so[slot, 256:768, :] = dot(r2[...], psq[:, cols])

            @pl.loop(0, ns // 2)
            def _(q):
                at = pl.multiple_of((1 - core) * 128 + q * 16, 16)
                hi, lo = two(so[slot, pl.ds(at, 16), :])
                asd[t, q, 0:16, :] = hi
                asd[t, q, 16:32, :] = lo
                asd[t, q, 32:48, :] = so[slot, pl.ds(at + 256, 16), :].astype(BF16)
                asd[t, q, 48:64, :] = so[slot, pl.ds(at + 512, 16), :].astype(BF16)

            a_copy(t).start()

        @pl.when((t > 0) & (t <= TILES))
        def _():
            stage1(t - 1)

        @pl.when(t >= LAG)
        def _():
            stage2(t - LAG)

    for low_part in range(2):
        x_across(low_part).wait_send()
        x_beside(low_part).wait_send()
        x_relay(low_part).wait_send()
    each(4, lambda i: block_at(i), lambda j: p_copy(j).wait_send())
    each(nz, zpeer, lambda j: b_copy(j).wait_send())
    each(nz, zpeer, lambda j: gr_copy(j).wait_send())
    for d in (1, 2, 3):
        c1(zpeer(d)).wait_send()
        c2(beside(d)).wait_send()
        f1(beside(d)).wait_send()
        f2(zpeer(d)).wait_send()
    each(nv, vpeer, lambda j: y_copy(j).wait_send())
    each(plane, ppeer, lambda j: v_copy(j).wait_send())

    for t in range(TILES):
        total = fin[t]
        if t % 2 == 0:
            x2(t).wait_recv()
            total = total + lrv[t, 0].astype(F32)
        else:
            for d in (1, 3, 2):
                z2_from(t, zpeer(d)).wait_recv()
                total = total + lrv[t, zpeer(d)].astype(F32)
        tot_ref[:, t * width : (t + 1) * width] = total

    for t in range(TILES):
        a_copy(t).wait_send()
        if t % 2 == 0:
            x2(t).wait_send()
            for d in (1, 2, 3):
                z1(t, zpeer(d)).wait_send()
        else:
            x1(t).wait_send()
            for d in (1, 2, 3):
                z2(t, zpeer(d)).wait_send()


def per_device(ns, nv, genotype, covariates, outcome, cohort, measured):
    vm = pltpu.VMEM
    dma = pltpu.SemaphoreType.DMA
    width = 2048 // TILES
    nz = ns // 4
    scratch = [
        vm((2048, 2048), BF16),
        vm((2048, 2048), BF16),
        vm((64, 8192), F32),
        vm((128, 8192), BF16),
        vm((2048, 256), BF16),
        vm((32, 2048), F32),
        vm((8, 8192), F32),
        vm((nv, 32, 2048), F32),
        vm((8, 8192), F32),
        vm((544, 8192), BF16),
        vm((544, 128), F32),
        vm((nz, 72, 128), F32),
        vm((nz, 72, 128), F32),
        vm((ns, 64, 128), F32),
        vm((ns, 64, 128), F32),
        vm((4, 64, 128), F32),
        vm((4, 64, 128), F32),
        vm((64, 128), F32),
        vm((nz, 64, 128), F32),
        vm((64, 128), F32),
        vm((8, 128), F32),
        vm((nz, 8, 128), F32),
        vm((8, 128), F32),
        vm((4 * nv, 8, 128), F32),
        vm((256, PROJ), BF16),
        vm((ns, 128, 128), BF16),
        vm((256, 2048), BF16),
        vm((512, 2048), BF16),
        vm((2, 768, width), F32),
        vm((TILES, ns // 2, 64, width), BF16),
        vm((TILES, ns // 2, 64, width), BF16),
        vm((TILES, ns // 2, 48, width), BF16),
        vm((TILES, ns // 2, 48, width), BF16),
        vm((TILES, 4, 48, width), F32),
        vm((TILES, 4, 48, width), BF16),
        vm((TILES, 4, 48, width), BF16),
        vm((TILES, 48, width), F32),
        dma,
    ]
    scratch += [dma((ns,))] * 4 + [dma((nz,))] * 6 + [dma((4,))] * 6 + [dma((nv,))] * 2
    scratch += [dma((4 * nv,))] * 2 + [dma((TILES,))] * 2 + [dma((TILES, ns // 2))] * 4
    scratch.append(pltpu.SemaphoreType.REGULAR)
    inside = pl.BlockSpec(memory_space=pltpu.VMEM)
    totals = pl.pallas_call(
        functools.partial(kernel, ns, nv),
        out_shape=jax.ShapeDtypeStruct((48, 2048), F32),
        in_specs=[pl.BlockSpec(memory_space=pl.ANY)] + [inside] * 4,
        out_specs=inside,
        scratch_shapes=scratch,
        compiler_params=pltpu.CompilerParams(
            collective_id=0, has_side_effects=True, vmem_limit_bytes=60 * 2**20
        ),
        name="score_tests",
    )(genotype, covariates.T, outcome.T, cohort[None, :], measured.T)
    score, robust, model = totals[0:16], totals[16:32], totals[32:48]
    return score * lax.rsqrt(robust + EPS), score * lax.rsqrt(model + EPS)


def solution(mesh):
    placed = (
        P("sample", "variant"),
        P("sample", None),
        P("sample", "variant"),
        P("sample"),
        P("variant", None),
    )
    return jax.shard_map(
        functools.partial(per_device, mesh.shape["sample"], mesh.shape["variant"]),
        mesh=mesh,
        in_specs=placed,
        out_specs=(P("sample", "variant"), P("sample", "variant")),
        check_vma=False,
    )
```
